512 devices in a mesh: seq: 128 (over z, y, x_lo), head: 4 (over x_hi, core).
Axes of the slice: x: 4 (x_hi: 2, x_lo: 2; x = x_hi * 2 + x_lo), y: 8, z: 8, core: 2. Of those that a mesh axis runs over, the one named last changes fastest.
Arguments:
- queries: bfloat16 [32768, 32, 128], P(('seq', 'head')), may hold values from -3 to 3
- key_vectors: bfloat16 [32768, 32, 128], P(('seq', 'head')), may hold values from -3 to 3
- value_vectors: bfloat16 [32768, 32, 128], P(('seq', 'head')), may hold values from -4 to 4
- grad_output: bfloat16 [32768, 32, 128], P(('seq', 'head')), may hold values from -4 to 4
- logsumexp: float32 [32, 32768], P('head', 'seq'), may hold values from 2 to 4
- row_delta: float32 [32, 32768], P('head', 'seq'), may hold values from -16 to 16
Outputs:
- grad_queries: bfloat16 [32768, 32, 128], P(('seq', 'head'))
- grad_keys: bfloat16 [32768, 32, 128], P(('seq', 'head'))
- grad_values: bfloat16 [32768, 32, 128], P(('seq', 'head'))
The draws below stay inside these ranges and needn't reach their ends.
All inputs are finite; a program needn't handle non-finite values.
Results may differ from the reference program's by a relative error of at most 0.02.
Values may be sent and summed in bfloat16 or wider, within the bound.
A program may use at most 64 MiB of HBM per device.

```python
import jax
import jax.numpy as jnp
from jax import lax

HEADS = 32
HEAD_DIM = 128
TOK_DEV = 256
STEPS = 4
TOKENS = 32768
N_SEQ = 128


def shard_levels(own_key, dims, pieces, smallest, high):
    def one(dim, parts):
        steps = jax.random.uniform(jax.random.fold_in(jax.random.fold_in(own_key, 6), dim), (parts,), jnp.float32, smallest / len(pieces), high / len(pieces))
        return jnp.repeat(jnp.exp(steps), dims[dim] // parts).reshape((-1,) + (1,) * (len(dims) - dim - 1))

    factor_of = one(*pieces[0])
    for cut in pieces[1:]:
        factor_of = factor_of * one(*cut)
    return factor_of


def gaussian(stream_key, shape, spread, bound, pieces=(), kind=jnp.bfloat16):
    array = jax.random.normal(stream_key, shape, jnp.float32) * spread
    if len(pieces) > 0:
        array = shard_levels(stream_key, shape, pieces, -0.22, 0.18) * array
    return jnp.clip(array, min=-bound, max=bound).astype(kind)


def setup_inputs(seed: int = 0) -> dict:
    seeds = jax.random.split(jax.random.key(seed), 7)
    return {
        "queries": gaussian(seeds[0], (TOKENS, HEADS, HEAD_DIM), 1.0, 3.0, ((0, 512),)),
        "key_vectors": gaussian(seeds[1], (TOKENS, HEADS, HEAD_DIM), 1.0, 3.0, ((0, 512),)),
        "value_vectors": gaussian(seeds[2], (TOKENS, HEADS, HEAD_DIM), 1.0, 4.0, ((0, 512),)),
        "grad_output": gaussian(seeds[3], (TOKENS, HEADS, HEAD_DIM), 1.0, 4.0, ((0, 512),)),
        "logsumexp": jnp.clip(2.0 + 2.0 * jax.random.uniform(seeds[4], (HEADS, TOKENS), jnp.float32) ** shard_levels(seeds[4], (HEADS, TOKENS), ((0, 4), (1, 128)), -0.2, 0.2), 2.0, 4.0),
        "row_delta": gaussian(seeds[5], (HEADS, TOKENS), 4.0, 16.0, ((0, 4), (1, 128)), jnp.float32),
    }


def token_places(device, seq_count, half_rows):
    offsets = jnp.arange(half_rows, dtype=jnp.int32)
    first = device * half_rows + offsets
    second = (2 * seq_count - 1 - device) * half_rows + offsets
    return jnp.concatenate([first, second]).astype(jnp.int32)


def rounded(values):
    return lax.optimization_barrier(values.astype(jnp.bfloat16)).astype(jnp.float32)


def tile_grads(q_rows, g_rows, lse_rows, delta_rows, k_rows, v_rows, causal, scaling):
    q_wide = q_rows.astype(jnp.float32)
    g_wide = g_rows.astype(jnp.float32)
    k_wide = k_rows.astype(jnp.float32)
    v_wide = v_rows.astype(jnp.float32)
    scores = jnp.einsum("qhd,khd->hqk", q_wide, k_wide) * scaling
    probs = jnp.where(causal[None], jnp.exp(scores - lse_rows[:, :, None]), 0.0)
    weights = rounded(probs)
    v_grad = jnp.einsum("hqk,qhd->khd", weights, g_wide)
    p_grad = jnp.einsum("qhd,khd->hqk", g_wide, v_wide)
    s_grad = rounded(probs * (p_grad - delta_rows[:, :, None]))
    q_grad = jnp.einsum("hqk,khd->qhd", s_grad, k_wide) * scaling
    k_grad = jnp.einsum("hqk,qhd->khd", s_grad, q_wide) * scaling
    return rounded(q_grad), rounded(k_grad), rounded(v_grad)


def reference(queries, key_vectors, value_vectors, grad_output, logsumexp, row_delta):
    seq_count = N_SEQ
    half_rows = TOK_DEV // 2
    scaling = HEAD_DIM ** -0.5
    block_shape = (seq_count, TOK_DEV, HEADS, HEAD_DIM)
    q_blocks = queries.reshape(block_shape)
    k_blocks = key_vectors.reshape(block_shape)
    v_blocks = value_vectors.reshape(block_shape)
    g_blocks = grad_output.reshape(block_shape)
    lse_blocks = logsumexp.reshape(HEADS, seq_count, TOK_DEV).transpose(1, 0, 2)
    delta_blocks = row_delta.reshape(HEADS, seq_count, TOK_DEV).transpose(1, 0, 2)
    zeros_total = jnp.zeros(block_shape, jnp.float32)

    def visit(index, carry):
        q_total, k_total, v_total = carry
        index = jnp.asarray(index).astype(jnp.int32)
        q_rows = q_blocks[index]
        g_rows = g_blocks[index]
        lse_rows = lse_blocks[index]
        delta_rows = delta_blocks[index]
        q_places = token_places(index, seq_count, half_rows)
        q_sum = jnp.zeros((TOK_DEV, HEADS, HEAD_DIM), jnp.float32)
        for distance in range(STEPS):
            source = ((index - distance) % seq_count).astype(jnp.int32)
            k_places = token_places(source, seq_count, half_rows)
            causal = k_places[None, :] <= q_places[:, None]
            q_part, k_part, v_part = tile_grads(q_rows, g_rows, lse_rows, delta_rows, k_blocks[source], v_blocks[source], causal, scaling)
            q_sum = q_sum + q_part
            k_total = k_total.at[source].add(k_part)
            v_total = v_total.at[source].add(v_part)
        q_total = q_total.at[index].set(q_sum)
        return q_total, k_total, v_total

    q_total, k_total, v_total = lax.fori_loop(0, seq_count, visit, (zeros_total, zeros_total, zeros_total))
    full_shape = (TOKENS, HEADS, HEAD_DIM)
    return (q_total.reshape(full_shape).astype(jnp.bfloat16), k_total.reshape(full_shape).astype(jnp.bfloat16), v_total.reshape(full_shape).astype(jnp.bfloat16))
```

```python
import math

import jax
import jax.numpy as jnp
from jax import lax
from jax.experimental import pallas as pl
from jax.experimental.pallas import tpu as pltpu
from jax.sharding import PartitionSpec as P

MESH = pl.DeviceIdType.MESH
GROUP = 8
BF16, F32 = jnp.bfloat16, jnp.float32
NT = (((1,), (1,)), ((), ()))
NN = (((1,), (0,)), ((), ()))
TN = (((0,), (0,)), ((), ()))


def dot(a, b, dims):
    return lax.dot_general(a, b, dims, preferred_element_type=F32)


def kernel(
    rows_total, q_ref, k_ref, v_ref, g_ref, lse_ref, delta_ref, dq_ref, dk_ref, dv_ref,
    wide, send_kv, send_qg, kv_buf, qg_buf, stats, halo, halo_grad, halo_in, acc,
    dq_buf, dkv_buf, fin_dq, fin_dkv, xq, xl, xacc, xdq, xd_in,
    s_kv, r_kv, s_qg, r_qg, s_st, r_st, s_hf, r_hf, s_hb, r_hb,
    s_dq, r_dq, s_dkv, r_dkv, s_xq, r_xq, s_xl, r_xl, s_xd, r_xd,
):
    rows, heads, dim = q_ref.shape
    hpg = heads // GROUP
    half = 2 * rows
    last = rows_total - 1
    scale = dim ** -0.5
    log2e = math.log2(math.e)

    s, h = lax.axis_index("seq"), lax.axis_index("head")
    lo, m = s % 2, s // 2
    hi, core = h // 2, h % 2
    place = lo * 4 + hi * 2 + core
    mine = hi * 4 + core * 2 + lo

    def peer(o):
        lo2, hi2, core2 = (lo + o % 2) % 2, (hi + o // 2 % 2) % 2, (core + o // 4) % 2
        return (2 * m + lo2, hi2 * 2 + core2), lo2 * 4 + hi2 * 2 + core2, hi2 * 4 + core2 * 2 + lo2

    peers = [(o, *peer(o)) for o in (2, 6, 3, 7, 1, 5, 4)]

    def row(step):
        return (2 * ((m + step + rows_total) % rows_total) + lo, h)

    def copy(src, dst, send, recv, to):
        return pltpu.make_async_remote_copy(
            src_ref=src, dst_ref=dst, send_sem=send, recv_sem=recv, device_id=to, device_id_type=MESH
        )

    def kv_copy(i, o, to, place2, mine2):
        return copy(send_kv.at[mine2, i], kv_buf.at[i, place], s_kv.at[i, o - 1], r_kv.at[i, o - 1], to)

    def qg_copy(i, o, to, place2, mine2):
        return copy(send_qg.at[mine2, i], qg_buf.at[i, place], s_qg.at[i, o - 1], r_qg.at[i, o - 1], to)

    def dq_copy(i, o, to, place2, mine2):
        return copy(dq_buf.at[i, place2], fin_dq.at[mine, i], s_dq.at[i, o - 1], r_dq.at[i, o - 1], to)

    def dkv_copy(i, o, to, place2, mine2):
        return copy(dkv_buf.at[i, place2], fin_dkv.at[mine, i], s_dkv.at[i, o - 1], r_dkv.at[i, o - 1], to)

    def stat_copy():
        return copy(stats.at[lo], stats.at[lo], s_st.at[0], r_st.at[0], peers[4][1])

    def halo_copy(i, n):
        first_half = kv_buf.at[i, pl.ds((4, 0, 4)[n], 2)]
        return copy(first_half, halo.at[i, n], s_hf.at[i, n], r_hf.at[i, n], row((2, 1, 1)[n]))

    def back_copy(i, n):
        return copy(halo_grad.at[i, n], halo_in.at[i, n], s_hb.at[i, n], r_hb.at[i, n], row((-2, -1, -1)[n]))

    def xq_copy(i, n):
        second_half = qg_buf.at[i, pl.ds((2, 2, 6)[n], 2)]
        slot = (2 * (m % 2), 0, 1)[n]
        return copy(second_half, xq.at[i, slot], s_xq.at[i, n], r_xq.at[i, slot], row((-2, -1, -1)[n]))

    def xq_arrived(i, slot):
        to = xq.at[i, slot]
        return copy(to, to, s_xq.at[i, 0], r_xq.at[i, slot], row(1))

    def xl_copy(n):
        slot = (m % 2, 0)[n]
        return copy(stats, xl.at[slot], s_xl.at[n], r_xl.at[slot], row((-2, -1)[n]))

    def xl_arrived(slot):
        return copy(xl.at[slot], xl.at[slot], s_xl.at[0], r_xl.at[slot], row(1))

    def xd_copy(i, n):
        slot = (0, 1, 2 * ((m - (rows_total - 2)) % 2))[n]
        return copy(xdq.at[i, slot], xd_in.at[i, n], s_xd.at[i, n], r_xd.at[i, n], row((1, 1, 2)[n]))

    barrier = pltpu.get_barrier_semaphore()
    for _, to, _, _ in peers:
        pl.semaphore_signal(barrier, inc=1, device_id=to, device_id_type=MESH)
    for step in (1, -1, 2, -2):
        pl.semaphore_signal(barrier, inc=1, device_id=row(step), device_id_type=MESH)

    def split_heads(src, dst, which):
        wide[...] = src[...].astype(F32).reshape(rows * heads, dim)
        for head in range(heads):
            dst[head // hpg, head % hpg, which] = wide[pl.ds(head, rows, stride=heads), :].astype(BF16)

    split_heads(k_ref, send_kv, 0)
    split_heads(v_ref, send_kv, 1)
    kv_buf[:, pl.ds(place, 1)] = send_kv[mine][:, None]
    stats[lo, 0] = lse_ref[...] * log2e
    stats[lo, 1] = delta_ref[...]

    pl.semaphore_wait(barrier, GROUP - 1 + 4)

    stat_copy().start()

    @pl.loop(0, hpg)
    def _(i):
        for p in peers:
            kv_copy(i, *p).start()

    split_heads(q_ref, send_qg, 0)
    split_heads(g_ref, send_qg, 1)
    qg_buf[:, pl.ds(place, 1)] = send_qg[mine][:, None]

    @pl.loop(0, hpg)
    def _(i):
        for p in peers:
            qg_copy(i, *p).start()

    @pl.when(m <= 1)
    def _():
        halo[:, 0] = jnp.zeros_like(halo[:, 0])

    @pl.when(m == 0)
    def _():
        halo[:, 1:3] = jnp.zeros_like(halo[:, 1:3])

    @pl.when(m >= last - 1)
    def _():
        halo_in[:, 0] = jnp.zeros_like(halo_in[:, 0])

    @pl.when(m == last)
    def _():
        halo_in[:, 1:3] = jnp.zeros_like(halo_in[:, 1:3])

    @pl.loop(0, hpg)
    def _(i):
        for p in peers:
            kv_copy(i, *p).wait_recv()

        @pl.when(m <= last - 2)
        def _():
            halo_copy(i, 0).start()

        @pl.when(m <= last - 1)
        def _():
            halo_copy(i, 1).start()
            halo_copy(i, 2).start()

    stat_copy().wait_recv()

    @pl.when(m <= 1)
    def _():
        xl_copy(0).start()

    @pl.when(m == 0)
    def _():
        xl_copy(1).start()

    key_at = lax.broadcasted_iota(jnp.int32, (half, half), 0)
    query_at = lax.broadcasted_iota(jnp.int32, (half, half), 1)
    causal = key_at <= query_at

    def flat(x):
        return x.reshape(-1, dim)

    def tile(kk, vv, qq, gg, lse, delta):
        scores = dot(kk, qq, NT) * (scale * log2e) - lse
        return jnp.exp2(scores), dot(vv, gg, NT) - delta

    def compute(i):
        keys = [halo[i, :, :, 0], kv_buf[i, 0:2, 0], kv_buf[i, 4:6, 0]]
        vals = [halo[i, :, :, 1], kv_buf[i, 0:2, 1], kv_buf[i, 4:6, 1]]
        keys = jnp.concatenate([flat(x) for x in keys], axis=0)
        vals = jnp.concatenate([flat(x) for x in vals], axis=0)
        at = pl.ds(4 * lo + i, 1)
        parts = []
        for b in range(2):
            kk, vv = keys[b * half : (b + 4) * half], vals[b * half : (b + 4) * half]
            k2, v2 = flat(kv_buf[i, 4 * b + 2 : 4 * b + 4, 0]), flat(kv_buf[i, 4 * b + 2 : 4 * b + 4, 1])
            qq, gg = flat(qg_buf[i, 4 * b : 4 * b + 4, 0]), flat(qg_buf[i, 4 * b : 4 * b + 4, 1])
            lse, delta = stats[b, 0, at, :], stats[b, 1, at, :]
            probs, pgrad = tile(kk, vv, qq, gg, lse, delta)
            own = probs[3 * half :]
            own = jnp.concatenate([jnp.where(causal, own[:, :half], 0.0), own[:, half:]], axis=1)
            probs = jnp.concatenate([probs[: 3 * half], own], axis=0)
            sgrad = (probs * pgrad).astype(BF16)
            dv = dot(probs.astype(BF16), gg, NN)
            dk = dot(sgrad, qq, NN) * scale
            q2, g2 = qq[half:], gg[half:]
            probs, pgrad = tile(k2, v2, q2, g2, lse[:, half:], delta[:, half:])
            probs = jnp.where(causal, probs, 0.0)
            sgrad2 = (probs * pgrad).astype(BF16)
            acc[i, b, 1, 1] = dot(probs.astype(BF16), g2, NN)
            acc[i, b, 1, 0] = dot(sgrad2, q2, NN) * scale
            dq = dot(sgrad, kk, TN)
            dq = jnp.concatenate([dq[:half], dq[half:] + dot(sgrad2, k2, TN)], axis=0) * scale
            dq_buf[i, 4 * b : 4 * b + 4] = dq.astype(BF16).reshape(4, rows, dim)
            parts.append((dk, dv))
        for which in range(2):
            e, o = parts[0][which], parts[1][which]
            halo_grad[i, 0, which] = e[:half].astype(BF16)
            halo_grad[i, 1, which] = (e[half : 2 * half] + o[:half]).astype(BF16)
            halo_grad[i, 2, which] = (e[2 * half : 3 * half] + o[half : 2 * half]).astype(BF16)
            acc[i, 0, 0, which] = e[3 * half :] + o[2 * half : 3 * half]
            acc[i, 1, 0, which] = o[3 * half :]

    def wrapped(i, slot, b, first):
        kk, vv = flat(kv_buf[i, 4 * b : 4 * b + 4, 0]), flat(kv_buf[i, 4 * b : 4 * b + 4, 1])
        qq, gg = flat(xq[i, slot, :, 0]), flat(xq[i, slot, :, 1])
        at = pl.ds(4 * lo + i, 1)
        lse = xl[slot // 2, slot % 2, 0, at, :][:, half:]
        delta = xl[slot // 2, slot % 2, 1, at, :][:, half:]
        probs, pgrad = tile(kk, vv, qq, gg, lse, delta)
        sgrad = (probs * pgrad).astype(BF16)
        dv = dot(probs.astype(BF16), gg, NN)
        dk = dot(sgrad, qq, NN) * scale
        for part in range(2):
            cut = slice(part * half, (part + 1) * half)
            acc[i, b, part, 0] += dk[cut]
            acc[i, b, part, 1] += dv[cut]
        dq = dot(sgrad, kk, TN) * scale
        if first:
            xacc[slot] = dq
        else:
            xacc[slot] += dq

    def send_dq(i):
        for p in peers:
            dq_copy(i, *p).start()

    def finish(i):
        @pl.when(m == last)
        def _():
            for slot in range(3):
                xq_arrived(i, slot).wait_recv()
            for slot in range(2):
                wrapped(i, slot, 0, True)
            wrapped(i, 2, 1, True)
            for slot in range(2):
                wrapped(i, slot, 1, False)
            xdq[i] = xacc[...].astype(BF16)
            for n in range(3):
                xd_copy(i, n).start()

        @pl.when(m == last - 1)
        def _():
            xq_arrived(i, 0).wait_recv()
            wrapped(i, 0, 1, True)
            xdq[i, 0] = xacc[0].astype(BF16)
            xd_copy(i, 2).start()

        @pl.when(m <= last - 2)
        def _():
            back_copy(i, 0).wait_recv()

        @pl.when(m <= last - 1)
        def _():
            back_copy(i, 1).wait_recv()
            back_copy(i, 2).wait_recv()

        for which in range(2):
            e = acc[i, 0, 0, which] + halo_in[i, 1, which].astype(F32)
            o = acc[i, 1, 0, which] + halo_in[i, 2, which].astype(F32) + halo_in[i, 0, which].astype(F32)
            for b, first in ((0, e), (1, o)):
                dkv_buf[i, 4 * b : 4 * b + 2, which] = first.astype(BF16).reshape(2, rows, dim)
                second = acc[i, b, 1, which]
                dkv_buf[i, 4 * b + 2 : 4 * b + 4, which] = second.astype(BF16).reshape(2, rows, dim)
        for p in peers:
            dkv_copy(i, *p).start()

        @pl.when(m <= 1)
        def _():
            xd_copy(i, 2).wait_recv()
            more = xd_in[i, 2].astype(F32).reshape(2, rows, dim)
            dq_buf[i, 2:4] = (dq_buf[i, 2:4].astype(F32) + more).astype(BF16)

        @pl.when(m == 0)
        def _():
            for slot in range(2):
                xd_copy(i, slot).wait_recv()
                at = slice(4 * slot + 2, 4 * slot + 4)
                more = xd_in[i, slot].astype(F32).reshape(2, rows, dim)
                dq_buf[i, at] = (dq_buf[i, at].astype(F32) + more).astype(BF16)

        @pl.when(m <= 1)
        def _():
            send_dq(i)

    @pl.when(m == last)
    def _():
        xl_arrived(0).wait_recv()
        xl_arrived(1).wait_recv()

    @pl.when(m == last - 1)
    def _():
        xl_arrived(0).wait_recv()

    @pl.loop(0, hpg)
    def _(i):
        for p in peers:
            qg_copy(i, *p).wait_recv()

        @pl.when(m <= 1)
        def _():
            xq_copy(i, 0).start()

        @pl.when(m == 0)
        def _():
            xq_copy(i, 1).start()
            xq_copy(i, 2).start()

        @pl.when(m >= 2)
        def _():
            halo_copy(i, 0).wait_recv()

        @pl.when(m >= 1)
        def _():
            halo_copy(i, 1).wait_recv()
            halo_copy(i, 2).wait_recv()

        compute(i)

        @pl.when(m >= 2)
        def _():
            back_copy(i, 0).start()

        @pl.when(m >= 1)
        def _():
            back_copy(i, 1).start()
            back_copy(i, 2).start()

        @pl.when(m >= 2)
        def _():
            send_dq(i)

        @pl.when(i >= 1)
        def _():
            finish(i - 1)

    finish(hpg - 1)

    @pl.loop(0, hpg)
    def _(i):
        for p in peers:
            dq_copy(i, *p).wait_recv()
        fin_dq[mine, i] = dq_buf[i, place]

    def join_heads(src, dst):
        for head in range(heads):
            wide[pl.ds(head, rows, stride=heads), :] = src(head // hpg, head % hpg).astype(F32)
        dst[...] = wide[...].reshape(rows, heads, dim).astype(BF16)

    join_heads(lambda j, i: fin_dq[j, i], dq_ref)

    @pl.loop(0, hpg)
    def _(i):
        for p in peers:
            dkv_copy(i, *p).wait_recv()
        fin_dkv[mine, i] = dkv_buf[i, place]

    join_heads(lambda j, i: fin_dkv[j, i, 0], dk_ref)
    join_heads(lambda j, i: fin_dkv[j, i, 1], dv_ref)

    stat_copy().wait_send()

    @pl.loop(0, hpg)
    def _(i):
        for p in peers:
            kv_copy(i, *p).wait_send()
            qg_copy(i, *p).wait_send()
            dq_copy(i, *p).wait_send()
            dkv_copy(i, *p).wait_send()

        @pl.when(m <= last - 2)
        def _():
            halo_copy(i, 0).wait_send()

        @pl.when(m <= last - 1)
        def _():
            halo_copy(i, 1).wait_send()
            halo_copy(i, 2).wait_send()

        @pl.when(m >= 2)
        def _():
            back_copy(i, 0).wait_send()

        @pl.when(m >= 1)
        def _():
            back_copy(i, 1).wait_send()
            back_copy(i, 2).wait_send()

        @pl.when(m <= 1)
        def _():
            xq_copy(i, 0).wait_send()

        @pl.when(m == 0)
        def _():
            xq_copy(i, 1).wait_send()
            xq_copy(i, 2).wait_send()

        @pl.when(m >= last - 1)
        def _():
            xd_copy(i, 2).wait_send()

        @pl.when(m == last)
        def _():
            xd_copy(i, 0).wait_send()
            xd_copy(i, 1).wait_send()

    @pl.when(m <= 1)
    def _():
        xl_copy(0).wait_send()

    @pl.when(m == 0)
    def _():
        xl_copy(1).wait_send()


def on_device(queries, key_vectors, value_vectors, grad_output, logsumexp, row_delta):
    rows, heads, dim = queries.shape
    hpg = heads // GROUP
    half = 2 * rows
    rows_total = lax.axis_size("seq") // 2
    vmem = pl.BlockSpec(memory_space=pltpu.VMEM)
    dma = pltpu.SemaphoreType.DMA
    out = jax.ShapeDtypeStruct((rows, heads, dim), BF16)

    def body(*refs):
        kernel(rows_total, *refs)

    return pl.pallas_call(
        body,
        out_shape=(out, out, out),
        in_specs=[vmem] * 6,
        out_specs=(vmem, vmem, vmem),
        scratch_shapes=[
            pltpu.VMEM((rows * heads, dim), F32),
            pltpu.VMEM((GROUP, hpg, 2, rows, dim), BF16),
            pltpu.VMEM((GROUP, hpg, 2, rows, dim), BF16),
            pltpu.VMEM((hpg, GROUP, 2, rows, dim), BF16),
            pltpu.VMEM((hpg, GROUP, 2, rows, dim), BF16),
            pltpu.VMEM((2, 2, *logsumexp.shape), F32),
            pltpu.VMEM((hpg, 3, 2, 2, rows, dim), BF16),
            pltpu.VMEM((hpg, 3, 2, half, dim), BF16),
            pltpu.VMEM((hpg, 3, 2, half, dim), BF16),
            pltpu.VMEM((hpg, 2, 2, 2, half, dim), F32),
            pltpu.VMEM((hpg, GROUP, rows, dim), BF16),
            pltpu.VMEM((hpg, GROUP, 2, rows, dim), BF16),
            pltpu.VMEM((GROUP, hpg, rows, dim), BF16),
            pltpu.VMEM((GROUP, hpg, 2, rows, dim), BF16),
            pltpu.VMEM((hpg, 3, 2, 2, rows, dim), BF16),
            pltpu.VMEM((2, 2, 2, *logsumexp.shape), F32),
            pltpu.VMEM((3, half, dim), F32),
            pltpu.VMEM((hpg, 3, half, dim), BF16),
            pltpu.VMEM((hpg, 3, half, dim), BF16),
            *[dma((hpg, GROUP - 1))] * 4,
            *[dma((1,))] * 2,
            *[dma((hpg, 3))] * 4,
            *[dma((hpg, GROUP - 1))] * 4,
            *[dma((hpg, 3))] * 2,
            *[dma((2,))] * 2,
            *[dma((hpg, 3))] * 2,
        ],
        compiler_params=pltpu.CompilerParams(
            collective_id=0, has_side_effects=True, vmem_limit_bytes=48 << 20
        ),
        name="window_grads",
    )(queries, key_vectors, value_vectors, grad_output, logsumexp, row_delta)


def solution(mesh):
    rows = P(("seq", "head"), None, None)
    stats = P("head", "seq")
    return jax.shard_map(
        on_device,
        mesh=mesh,
        in_specs=(rows, rows, rows, rows, stats, stats),
        out_specs=(rows, rows, rows),
        check_vma=False,
    )
```

```python
import math

import jax
import jax.numpy as jnp
from jax import lax
from jax.experimental import pallas as pl
from jax.experimental.pallas import tpu as pltpu
from jax.sharding import PartitionSpec as P

MESH = pl.DeviceIdType.MESH
GROUP = 8
BF16, F32 = jnp.bfloat16, jnp.float32
NT = (((1,), (1,)), ((), ()))
NN = (((1,), (0,)), ((), ()))
TN = (((0,), (0,)), ((), ()))


def dot(a, b, dims):
    return lax.dot_general(a, b, dims, preferred_element_type=F32)


def kernel(
    rows_total, q_ref, k_ref, v_ref, g_ref, lse_ref, delta_ref, fin_dq, fin_dkv,
    send_kv, send_qg, kv_buf, qg_buf, stats, halo, halo_grad, halo_in, acc,
    dq_buf, dkv_buf, xq, xl, xacc, xdq, xd_in, chain, local, local_stats, ready, s_in, s_own,
    s_kv, r_kv, s_qg, r_qg, s_st, r_st, s_hf, r_hf, s_hb, r_hb,
    s_dq, r_dq, s_dkv, r_dkv, s_xq, r_xq, s_xl, r_xl, s_xd, r_xd,
):
    rows, heads, dim = q_ref.shape
    hpg = heads // GROUP
    half = 2 * rows
    last = rows_total - 1
    scale = dim ** -0.5
    log2e = math.log2(math.e)

    s, h = lax.axis_index("seq"), lax.axis_index("head")
    lo, m = s % 2, s // 2
    hi, core = h // 2, h % 2
    place = lo * 4 + hi * 2 + core
    mine = hi * 4 + core * 2 + lo

    def peer(o):
        lo2, hi2, core2 = (lo + o % 2) % 2, (hi + o // 2 % 2) % 2, (core + o // 4) % 2
        return (2 * m + lo2, hi2 * 2 + core2), lo2 * 4 + hi2 * 2 + core2, hi2 * 4 + core2 * 2 + lo2

    peers = [(o, *peer(o)) for o in (2, 6, 3, 7, 1, 5, 4)]

    def row(step):
        return (2 * ((m + step + rows_total) % rows_total) + lo, h)

    def copy(src, dst, send, recv, to):
        return pltpu.make_async_remote_copy(
            src_ref=src, dst_ref=dst, send_sem=send, recv_sem=recv, device_id=to, device_id_type=MESH
        )

    def kv_copy(i, o, to, place2, mine2):
        return copy(send_kv.at[mine2, i], kv_buf.at[i, place], s_kv.at[i, o - 1], r_kv.at[i, o - 1], to)

    def qg_copy(i, o, to, place2, mine2):
        return copy(send_qg.at[mine2, i], qg_buf.at[i, place], s_qg.at[i, o - 1], r_qg.at[i, o - 1], to)

    def dq_copy(i, o, to, place2, mine2):
        return copy(dq_buf.at[i, place2], fin_dq.at[mine, i], s_dq.at[i, o - 1], r_dq.at[i, o - 1], to)

    def dkv_copy(i, o, to, place2, mine2):
        return copy(dkv_buf.at[i, place2], fin_dkv.at[mine, i], s_dkv.at[i, o - 1], r_dkv.at[i, o - 1], to)

    def keep(i):
        return (
            pltpu.make_async_copy(dq_buf.at[i, place], fin_dq.at[mine, i], s_own.at[i, 0]),
            pltpu.make_async_copy(dkv_buf.at[i, place], fin_dkv.at[mine, i], s_own.at[i, 1]),
        )

    def stat_copy():
        return copy(stats.at[lo], stats.at[lo], s_st.at[0], r_st.at[0], peers[4][1])

    def halo_copy(i, n):
        src = halo.at[i, 2] if n == 0 else kv_buf.at[i, pl.ds((0, 4)[n - 1], 2)]
        return copy(src, halo.at[i, n], s_hf.at[i, n], r_hf.at[i, n], row(1))

    def back_copy(i, n):
        return copy(halo_grad.at[i, n], halo_in.at[i, n], s_hb.at[i, n], r_hb.at[i, n], row(-1))

    def xq_copy(i, slot):
        second_half = qg_buf.at[i, pl.ds((2, 6, 2)[slot], 2)]
        return copy(second_half, xq.at[i, slot], s_xq.at[i, slot], r_xq.at[i, slot], row((-1, -1, -2)[slot]))

    def xq_hand_on(i):
        return copy(xq.at[i, 0], xq.at[i, 0], s_xq.at[i, 0], r_xq.at[i, 0], row(-1))

    def xq_arrived(i, slot):
        to = xq.at[i, slot]
        return copy(to, to, s_xq.at[i, 0], r_xq.at[i, slot], row(1))

    def xl_copy(n):
        slot = (m % 2, 0)[n]
        return copy(stats, xl.at[slot], s_xl.at[n], r_xl.at[slot], row((-2, -1)[n]))

    def xl_arrived(slot):
        return copy(xl.at[slot], xl.at[slot], s_xl.at[0], r_xl.at[slot], row(1))

    def xd_copy(i, n):
        slot = (0, 1, 2 * ((m - (rows_total - 2)) % 2))[n]
        return copy(xdq.at[i, slot], xd_in.at[i, n], s_xd.at[i, n], r_xd.at[i, n], row((1, 1, 2)[n]))

    loads = [pltpu.make_async_copy(src, local.at[n], s_in.at[n]) for n, src in enumerate((k_ref, v_ref, q_ref, g_ref))]
    stat_loads = [
        pltpu.make_async_copy(src, local_stats.at[n], s_in.at[4 + n]) for n, src in enumerate((lse_ref, delta_ref))
    ]
    for load in loads[:2] + stat_loads + loads[2:]:
        load.start()

    barrier = pltpu.get_barrier_semaphore()
    for _, to, _, _ in peers:
        pl.semaphore_signal(barrier, inc=1, device_id=to, device_id_type=MESH)

    def tell(sem, step):
        pl.semaphore_signal(sem, inc=1, device_id=row(step), device_id_type=MESH)

    @pl.when(m <= last - 1)
    def _():
        tell(barrier, 1)

    @pl.when(m >= 1)
    def _():
        tell(barrier, -1)

    @pl.when(m <= 1)
    def _():
        tell(barrier, -2)

    @pl.when(m == 0)
    def _():
        tell(barrier, -1)

    def split_heads(n, dst, which):
        loads[n].wait()
        dst[:, :, which] = jnp.swapaxes(local[n], 0, 1).reshape(GROUP, hpg, rows, dim)

    split_heads(0, send_kv, 0)
    split_heads(1, send_kv, 1)
    kv_buf[:, pl.ds(place, 1)] = send_kv[mine][:, None]
    for load in stat_loads:
        load.wait()
    stats[lo, 0] = local_stats[0] * log2e
    stats[lo, 1] = local_stats[1]

    one, none = jnp.int32(1), jnp.int32(0)
    along = jnp.where(m >= 1, one, none) + jnp.where(m <= last - 1, one, none)
    ends = jnp.where(m >= last - 1, one, none) + jnp.where(m == last, one, none)
    pl.semaphore_wait(barrier, GROUP - 1 + along + ends)

    @pl.when(m >= last - 1)
    def _():
        tell(ready, 2)

    @pl.when(m == last)
    def _():
        tell(ready, 1)

    stat_copy().start()

    def send(what, first, count):
        @pl.loop(first, first + count)
        def _(i):
            for p in peers:
                what(i, *p).start()

    send(kv_copy, 0, 2)
    split_heads(2, send_qg, 0)
    split_heads(3, send_qg, 1)
    qg_buf[:, pl.ds(place, 1)] = send_qg[mine][:, None]

    @pl.loop(0, hpg - 2)
    def _(i):
        for p in peers:
            qg_copy(i, *p).start()
        for p in peers:
            kv_copy(i + 2, *p).start()

    send(qg_copy, hpg - 2, 2)

    @pl.when(m <= 1)
    def _():
        halo[:, 0] = jnp.zeros_like(halo[:, 0])

    @pl.when(m == 0)
    def _():
        halo[:, 1:3] = jnp.zeros_like(halo[:, 1:3])

    @pl.when(m == last)
    def _():
        halo_in[...] = jnp.zeros_like(halo_in)

    def hand_on(i):
        @pl.when(m >= 1)
        def _():
            halo_copy(i, 2).wait_recv()

            @pl.when(m <= last - 1)
            def _():
                halo_copy(i, 0).start()

    def share_keys(i):
        for p in peers:
            kv_copy(i, *p).wait_recv()

        @pl.when(m <= last - 1)
        def _():
            halo_copy(i, 2).start()
            halo_copy(i, 1).start()

    @pl.loop(0, 2)
    def _(i):
        share_keys(i)

    @pl.loop(0, 2)
    def _(i):
        hand_on(i)

    stat_copy().wait_recv()

    @pl.when(m <= 1)
    def _():
        pl.semaphore_wait(ready, 2 - m)
        xl_copy(0).start()

    @pl.when(m == 0)
    def _():
        xl_copy(1).start()

    key_at = lax.broadcasted_iota(jnp.int32, (half, half), 0)
    query_at = lax.broadcasted_iota(jnp.int32, (half, half), 1)
    causal = key_at <= query_at

    def flat(x):
        return x.reshape(-1, dim)

    def tile(kk, vv, qq, gg, lse, delta):
        scores = dot(kk, qq, NT) * (scale * log2e) - lse
        return jnp.exp2(scores), dot(vv, gg, NT) - delta

    def compute(i):
        keys = [halo[i, :, :, 0], kv_buf[i, 0:2, 0], kv_buf[i, 4:6, 0]]
        vals = [halo[i, :, :, 1], kv_buf[i, 0:2, 1], kv_buf[i, 4:6, 1]]
        keys = jnp.concatenate([flat(x) for x in keys], axis=0)
        vals = jnp.concatenate([flat(x) for x in vals], axis=0)
        at = pl.ds(4 * lo + i, 1)
        parts = []
        for b in range(2):
            kk, vv = keys[b * half : (b + 4) * half], vals[b * half : (b + 4) * half]
            k2, v2 = flat(kv_buf[i, 4 * b + 2 : 4 * b + 4, 0]), flat(kv_buf[i, 4 * b + 2 : 4 * b + 4, 1])
            qq, gg = flat(qg_buf[i, 4 * b : 4 * b + 4, 0]), flat(qg_buf[i, 4 * b : 4 * b + 4, 1])
            lse, delta = stats[b, 0, at, :], stats[b, 1, at, :]
            probs, pgrad = tile(kk, vv, qq, gg, lse, delta)
            own = probs[3 * half :]
            own = jnp.concatenate([jnp.where(causal, own[:, :half], 0.0), own[:, half:]], axis=1)
            probs = jnp.concatenate([probs[: 3 * half], own], axis=0)
            sgrad = (probs * pgrad).astype(BF16)
            dv = dot(probs.astype(BF16), gg, NN)
            dk = dot(sgrad, qq, NN) * scale
            q2, g2 = qq[half:], gg[half:]
            probs, pgrad = tile(k2, v2, q2, g2, lse[:, half:], delta[:, half:])
            probs = jnp.where(causal, probs, 0.0)
            sgrad2 = (probs * pgrad).astype(BF16)
            acc[i, b, 1, 1] = dot(probs.astype(BF16), g2, NN)
            acc[i, b, 1, 0] = dot(sgrad2, q2, NN) * scale
            dq = dot(sgrad, kk, TN)
            dq = jnp.concatenate([dq[:half], dq[half:] + dot(sgrad2, k2, TN)], axis=0) * scale
            dq_buf[i, 4 * b : 4 * b + 4] = dq.astype(BF16).reshape(4, rows, dim)
            parts.append((dk, dv))
        for which in range(2):
            e, o = parts[0][which], parts[1][which]
            halo_grad[i, 0, which] = e[:half].astype(BF16)
            halo_grad[i, 1, which] = (e[half : 2 * half] + o[:half]).astype(BF16)
            chain[i, which] = e[2 * half : 3 * half] + o[half : 2 * half]
            acc[i, 0, 0, which] = e[3 * half :] + o[2 * half : 3 * half]
            acc[i, 1, 0, which] = o[3 * half :]

    def wrapped(i, slot, b, first):
        kk, vv = flat(kv_buf[i, 4 * b : 4 * b + 4, 0]), flat(kv_buf[i, 4 * b : 4 * b + 4, 1])
        qq, gg = flat(xq[i, slot, :, 0]), flat(xq[i, slot, :, 1])
        at = pl.ds(4 * lo + i, 1)
        lse = xl[slot // 2, slot % 2, 0, at, :][:, half:]
        delta = xl[slot // 2, slot % 2, 1, at, :][:, half:]
        probs, pgrad = tile(kk, vv, qq, gg, lse, delta)
        sgrad = (probs * pgrad).astype(BF16)
        dv = dot(probs.astype(BF16), gg, NN)
        dk = dot(sgrad, qq, NN) * scale
        for part in range(2):
            cut = slice(part * half, (part + 1) * half)
            acc[i, b, part, 0] += dk[cut]
            acc[i, b, part, 1] += dv[cut]
        dq = dot(sgrad, kk, TN) * scale
        if first:
            xacc[slot] = dq
        else:
            xacc[slot] += dq

    def send_dq(i):
        for p in peers:
            dq_copy(i, *p).start()

    def pass_back(i):
        @pl.when(m >= 1)
        def _():
            @pl.when(m <= last - 1)
            def _():
                back_copy(i, 0).wait_recv()

            halo_grad[i, 2] = (chain[i] + halo_in[i, 0].astype(F32)).astype(BF16)
            back_copy(i, 2).start()

    def wrapped_pairs(i):
        @pl.when(m == last)
        def _():
            xq_arrived(i, 1).wait_recv()
            xq_arrived(i, 2).wait_recv()
            for slot in range(2):
                wrapped(i, slot, 0, True)
            wrapped(i, 2, 1, True)
            for slot in range(2):
                wrapped(i, slot, 1, False)
            xdq[i] = xacc[...].astype(BF16)
            for n in range(3):
                xd_copy(i, n).start()

        @pl.when(m == last - 1)
        def _():
            xq_arrived(i, 0).wait_recv()
            wrapped(i, 0, 1, True)
            xdq[i, 0] = xacc[0].astype(BF16)
            xd_copy(i, 2).start()

    def finish(i):
        @pl.when(m <= last - 1)
        def _():
            back_copy(i, 1).wait_recv()
            back_copy(i, 2).wait_recv()

        for which in range(2):
            for b in range(2):
                first = acc[i, b, 0, which] + halo_in[i, 1 + b, which].astype(F32)
                dkv_buf[i, 4 * b : 4 * b + 2, which] = first.astype(BF16).reshape(2, rows, dim)
                second = acc[i, b, 1, which]
                dkv_buf[i, 4 * b + 2 : 4 * b + 4, which] = second.astype(BF16).reshape(2, rows, dim)
        for p in peers:
            dkv_copy(i, *p).start()

    def finish_first(i):
        xd_copy(i, 2).wait_recv()
        more = xd_in[i, 2].astype(F32).reshape(2, rows, dim)
        dq_buf[i, 2:4] = (dq_buf[i, 2:4].astype(F32) + more).astype(BF16)

        @pl.when(m == 0)
        def _():
            for slot in range(2):
                xd_copy(i, slot).wait_recv()
                at = slice(4 * slot + 2, 4 * slot + 4)
                more = xd_in[i, slot].astype(F32).reshape(2, rows, dim)
                dq_buf[i, at] = (dq_buf[i, at].astype(F32) + more).astype(BF16)

        send_dq(i)

    @pl.when(m == last)
    def _():
        xl_arrived(0).wait_recv()
        xl_arrived(1).wait_recv()

    @pl.when(m == last - 1)
    def _():
        xl_arrived(0).wait_recv()

    def grads(i):
        for p in peers:
            qg_copy(i, *p).wait_recv()

        @pl.when(m == 0)
        def _():
            xq_copy(i, 0).start()
            xq_copy(i, 1).start()

        @pl.when(m == 1)
        def _():
            xq_copy(i, 2).start()

        @pl.when(m >= 2)
        def _():
            halo_copy(i, 0).wait_recv()

        @pl.when(m >= 1)
        def _():
            halo_copy(i, 1).wait_recv()

        compute(i)

        @pl.when(m >= 2)
        def _():
            back_copy(i, 0).start()

        @pl.when(m >= 1)
        def _():
            back_copy(i, 1).start()

        @pl.when(m >= 2)
        def _():
            send_dq(i)

    @pl.loop(0, hpg)
    def _(i):
        @pl.when(m == last)
        def _():
            xq_arrived(i, 0).wait_recv()
            xq_hand_on(i).start()

        grads(i)

        @pl.when((i >= 1) & (i + 1 < hpg))
        def _():
            hand_on(i + 1)

        @pl.when(i >= 1)
        def _():
            pass_back(i - 1)

        @pl.when(i + 2 < hpg)
        def _():
            share_keys(i + 2)

        @pl.when(i >= 1)
        def _():
            wrapped_pairs(i - 1)

    @pl.loop(0, hpg)
    def _(i):
        finish(i)

        @pl.when(i == 1)
        def _():
            pass_back(hpg - 1)
            wrapped_pairs(hpg - 1)

        @pl.when((m <= 1) & (i >= 2))
        def _():
            finish_first(i - 2)

    @pl.when(m <= 1)
    def _():
        @pl.loop(hpg - 2, hpg)
        def _(i):
            finish_first(i)

    @pl.loop(0, hpg)
    def _(i):
        own_dq, own_dkv = keep(i)
        own_dq.start()
        own_dkv.start()

    @pl.loop(0, hpg)
    def _(i):
        for p in peers:
            dq_copy(i, *p).wait_recv()
            dkv_copy(i, *p).wait_recv()
        own_dq, own_dkv = keep(i)
        own_dq.wait()
        own_dkv.wait()

    stat_copy().wait_send()

    @pl.loop(0, hpg)
    def _(i):
        for p in peers:
            kv_copy(i, *p).wait_send()
            qg_copy(i, *p).wait_send()
            dq_copy(i, *p).wait_send()
            dkv_copy(i, *p).wait_send()

        @pl.when(m <= last - 1)
        def _():
            halo_copy(i, 1).wait_send()
            halo_copy(i, 2).wait_send()

            @pl.when(m >= 1)
            def _():
                halo_copy(i, 0).wait_send()

        @pl.when(m >= 2)
        def _():
            back_copy(i, 0).wait_send()

        @pl.when(m >= 1)
        def _():
            back_copy(i, 1).wait_send()
            back_copy(i, 2).wait_send()

        @pl.when(m == 0)
        def _():
            xq_copy(i, 0).wait_send()
            xq_copy(i, 1).wait_send()

        @pl.when(m == 1)
        def _():
            xq_copy(i, 2).wait_send()

        @pl.when(m == last)
        def _():
            xq_hand_on(i).wait_send()

        @pl.when(m >= last - 1)
        def _():
            xd_copy(i, 2).wait_send()

        @pl.when(m == last)
        def _():
            xd_copy(i, 0).wait_send()
            xd_copy(i, 1).wait_send()

    @pl.when(m <= 1)
    def _():
        xl_copy(0).wait_send()

    @pl.when(m == 0)
    def _():
        xl_copy(1).wait_send()


def on_device(queries, key_vectors, value_vectors, grad_output, logsumexp, row_delta):
    rows, heads, dim = queries.shape
    hpg = heads // GROUP
    half = 2 * rows
    rows_total = lax.axis_size("seq") // 2
    hbm = pl.BlockSpec(memory_space=pl.ANY)
    dma = pltpu.SemaphoreType.DMA
    dq_shape = jax.ShapeDtypeStruct((GROUP, hpg, rows, dim), BF16)
    dkv_shape = jax.ShapeDtypeStruct((GROUP, hpg, 2, rows, dim), BF16)

    def body(*refs):
        kernel(rows_total, *refs)

    dq, dkv = pl.pallas_call(
        body,
        out_shape=(dq_shape, dkv_shape),
        in_specs=[hbm] * 6,
        out_specs=(hbm, hbm),
        scratch_shapes=[
            pltpu.VMEM((GROUP, hpg, 2, rows, dim), BF16),
            pltpu.VMEM((GROUP, hpg, 2, rows, dim), BF16),
            pltpu.VMEM((hpg, GROUP, 2, rows, dim), BF16),
            pltpu.VMEM((hpg, GROUP, 2, rows, dim), BF16),
            pltpu.VMEM((2, 2, *logsumexp.shape), F32),
            pltpu.VMEM((hpg, 3, 2, 2, rows, dim), BF16),
            pltpu.VMEM((hpg, 3, 2, half, dim), BF16),
            pltpu.VMEM((hpg, 3, 2, half, dim), BF16),
            pltpu.VMEM((hpg, 2, 2, 2, half, dim), F32),
            pltpu.VMEM((hpg, GROUP, rows, dim), BF16),
            pltpu.VMEM((hpg, GROUP, 2, rows, dim), BF16),
            pltpu.VMEM((hpg, 3, 2, 2, rows, dim), BF16),
            pltpu.VMEM((2, 2, 2, *logsumexp.shape), F32),
            pltpu.VMEM((3, half, dim), F32),
            pltpu.VMEM((hpg, 3, half, dim), BF16),
            pltpu.VMEM((hpg, 3, half, dim), BF16),
            pltpu.VMEM((hpg, 2, half, dim), F32),
            pltpu.VMEM((4, rows, heads, dim), BF16),
            pltpu.VMEM((2, *logsumexp.shape), F32),
            pltpu.SemaphoreType.REGULAR,
            dma((6,)),
            dma((hpg, 2)),
            *[dma((hpg, GROUP - 1))] * 4,
            *[dma((1,))] * 2,
            *[dma((hpg, 3))] * 4,
            *[dma((hpg, GROUP - 1))] * 4,
            *[dma((hpg, 3))] * 2,
            *[dma((2,))] * 2,
            *[dma((hpg, 3))] * 2,
        ],
        compiler_params=pltpu.CompilerParams(
            collective_id=0, has_side_effects=True, vmem_limit_bytes=60 << 20
        ),
        name="window_grads",
    )(queries, key_vectors, value_vectors, grad_output, logsumexp, row_delta)

    def by_row(x):
        return jnp.swapaxes(x.reshape(heads, rows, dim), 0, 1)

    return by_row(dq), by_row(dkv[:, :, 0]), by_row(dkv[:, :, 1])


def solution(mesh):
    rows = P(("seq", "head"), None, None)
    stats = P("head", "seq")
    return jax.shard_map(
        on_device,
        mesh=mesh,
        in_specs=(rows, rows, rows, rows, stats, stats),
        out_specs=(rows, rows, rows),
        check_vma=False,
    )
```

```python
import math

import jax
import jax.numpy as jnp
from jax import lax
from jax.experimental import pallas as pl
from jax.experimental.pallas import tpu as pltpu
from jax.sharding import PartitionSpec as P

MESH = pl.DeviceIdType.MESH
GROUP = 8
BF16, F32 = jnp.bfloat16, jnp.float32
NT = (((1,), (1,)), ((), ()))
NN = (((1,), (0,)), ((), ()))
TN = (((0,), (0,)), ((), ()))


def dot(a, b, dims):
    return lax.dot_general(a, b, dims, preferred_element_type=F32)


def kernel(
    rows_total, q_ref, k_ref, v_ref, g_ref, lse_ref, delta_ref, fin_dq, fin_dkv,
    sent, got, stats, halo, halo_grad, halo_in, acc,
    dq_buf, dkv_buf, xq, xl, xacc, xdq, xd_in, chain, local, local_stats, ready, s_in, s_own,
    s_split, r_split, s_st, r_st, s_hf, r_hf, s_hb, r_hb,
    s_dq, r_dq, s_dkv, r_dkv, s_xq, r_xq, s_xl, r_xl, s_xd, r_xd,
):
    rows, heads, dim = q_ref.shape
    hpg = heads // GROUP
    half = 2 * rows
    last = rows_total - 1
    scale = dim ** -0.5
    log2e = math.log2(math.e)

    s, h = lax.axis_index("seq"), lax.axis_index("head")
    lo, m = s % 2, s // 2
    hi, core = h // 2, h % 2
    place = lo * 4 + hi * 2 + core
    mine = hi * 4 + core * 2 + lo

    def peer(o):
        lo2, hi2, core2 = (lo + o % 2) % 2, (hi + o // 2 % 2) % 2, (core + o // 4) % 2
        return (2 * m + lo2, hi2 * 2 + core2), lo2 * 4 + hi2 * 2 + core2, hi2 * 4 + core2 * 2 + lo2

    peers = [(o, *peer(o)) for o in (2, 6, 3, 7, 1, 5, 4)]

    def row(step):
        return (2 * ((m + step + rows_total) % rows_total) + lo, h)

    def copy(src, dst, send, recv, to):
        return pltpu.make_async_remote_copy(
            src_ref=src, dst_ref=dst, send_sem=send, recv_sem=recv, device_id=to, device_id_type=MESH
        )

    kv_buf, qg_buf = got.at[0], got.at[1]

    def split_copy(kind, i, o, to, place2, mine2):
        return copy(
            sent.at[kind, mine2, i], got.at[kind, i, place], s_split.at[kind, i, o - 1], r_split.at[kind, i, o - 1], to
        )

    def split_arrived(kind, i, part):
        @pl.when(hi == part)
        def _():
            for p in peers:
                if p[0] in (1, 4, 5):
                    split_copy(kind, i, *p).wait_recv()

        @pl.when(hi != part)
        def _():
            for p in peers:
                if p[0] not in (1, 4, 5):
                    split_copy(kind, i, *p).wait_recv()

    def dq_copy(i, o, to, place2, mine2):
        return copy(dq_buf.at[i, place2], fin_dq.at[mine, i], s_dq.at[i, o - 1], r_dq.at[i, o - 1], to)

    def dkv_copy(i, o, to, place2, mine2):
        return copy(dkv_buf.at[i, place2], fin_dkv.at[mine, i], s_dkv.at[i, o - 1], r_dkv.at[i, o - 1], to)

    def keep(i):
        return (
            pltpu.make_async_copy(dq_buf.at[i, place], fin_dq.at[mine, i], s_own.at[i, 0]),
            pltpu.make_async_copy(dkv_buf.at[i, place], fin_dkv.at[mine, i], s_own.at[i, 1]),
        )

    def stat_copy():
        return copy(stats.at[lo], stats.at[lo], s_st.at[0], r_st.at[0], peers[4][1])

    def halo_copy(i, n):
        src = halo.at[i, 2] if n == 0 else kv_buf.at[i, pl.ds((0, 4)[n - 1], 2)]
        return copy(src, halo.at[i, n], s_hf.at[i, n], r_hf.at[i, n], row(1))

    def back_copy(i, n):
        return copy(halo_grad.at[i, n], halo_in.at[i, n], s_hb.at[i, n], r_hb.at[i, n], row(-1))

    def xq_copy(i, n):
        second_half = qg_buf.at[i, pl.ds((2, 6, 2)[n], 2)]
        slot = (0, 1, 2 * (m % 2))[n]
        return copy(second_half, xq.at[i, slot], s_xq.at[i, n], r_xq.at[i, slot], row((-1, -1, -2)[n]))

    def xq_arrived(i, slot):
        to = xq.at[i, slot]
        return copy(to, to, s_xq.at[i, 0], r_xq.at[i, slot], row(1))

    def xl_copy(n):
        slot = (m % 2, 0)[n]
        return copy(stats, xl.at[slot], s_xl.at[n], r_xl.at[slot], row((-2, -1)[n]))

    def xl_arrived(slot):
        return copy(xl.at[slot], xl.at[slot], s_xl.at[0], r_xl.at[slot], row(1))

    def xd_copy(i, n):
        slot = (0, 1, 2 * ((m - (rows_total - 2)) % 2))[n]
        return copy(xdq.at[i, slot], xd_in.at[i, n], s_xd.at[i, n], r_xd.at[i, n], row((1, 1, 2)[n]))

    def load_of(n, src=k_ref):
        return pltpu.make_async_copy(src, local.at[n], s_in.at[n])

    stat_loads = [
        pltpu.make_async_copy(src, local_stats.at[n], s_in.at[4 + n]) for n, src in enumerate((lse_ref, delta_ref))
    ]
    for n, src in enumerate((k_ref, v_ref, q_ref, g_ref)):
        load_of(n, src).start()
    for load in stat_loads:
        load.start()

    barrier = pltpu.get_barrier_semaphore()
    for _, to, _, _ in peers:
        pl.semaphore_signal(barrier, inc=1, device_id=to, device_id_type=MESH)

    def tell(sem, step):
        pl.semaphore_signal(sem, inc=1, device_id=row(step), device_id_type=MESH)

    @pl.when(m <= last - 1)
    def _():
        tell(barrier, 1)

    @pl.when(m >= 1)
    def _():
        tell(barrier, -1)

    @pl.when(m <= 1)
    def _():
        tell(barrier, -2)

    @pl.when(m == 0)
    def _():
        tell(barrier, -1)

    def split_heads(kind):
        for which in range(2):
            load_of(2 * kind + which).wait()
            by_head = jnp.swapaxes(local[2 * kind + which], 0, 1)
            sent[kind, :, :, which] = by_head.reshape(GROUP, hpg, rows, dim)
        got[kind, :, pl.ds(place, 1)] = sent[kind, mine][:, None]

    first, second = hi, 1 - hi
    split_heads(first)
    for load in stat_loads:
        load.wait()
    stats[lo, 0] = local_stats[0] * log2e
    stats[lo, 1] = local_stats[1]

    one, none = jnp.int32(1), jnp.int32(0)
    along = jnp.where(m >= 1, one, none) + jnp.where(m <= last - 1, one, none)
    ends = jnp.where(m >= last - 1, one, none) + jnp.where(m == last, one, none)
    pl.semaphore_wait(barrier, GROUP - 1 + along + ends)

    @pl.when(m >= last - 1)
    def _():
        tell(ready, 2)

    @pl.when(m == last)
    def _():
        tell(ready, 1)

    stat_copy().start()

    def send(kind, i):
        for p in peers:
            split_copy(kind, i, *p).start()

    @pl.loop(0, 2)
    def _(i):
        send(first, i)

    split_heads(second)

    @pl.loop(0, hpg - 2)
    def _(i):
        send(second, i)
        send(first, i + 2)

    @pl.loop(hpg - 2, hpg)
    def _(i):
        send(second, i)

    acc[...] = jnp.zeros_like(acc)

    @pl.when(m <= 1)
    def _():
        halo[:, 0] = jnp.zeros_like(halo[:, 0])

    @pl.when(m == 0)
    def _():
        halo[:, 1:3] = jnp.zeros_like(halo[:, 1:3])

    @pl.when(m == last)
    def _():
        halo_in[...] = jnp.zeros_like(halo_in)

    def hand_on(i):
        @pl.when(m >= 1)
        def _():
            halo_copy(i, 2).wait_recv()

            @pl.when(m <= last - 1)
            def _():
                halo_copy(i, 0).start()

    def share(i):
        split_arrived(0, i, 0)

        @pl.when(m <= last - 1)
        def _():
            halo_copy(i, 2).start()
            halo_copy(i, 1).start()

        split_arrived(1, i, 1)

        @pl.when(m == 0)
        def _():
            xq_copy(i, 0).start()
            xq_copy(i, 1).start()

        @pl.when(m <= 1)
        def _():
            xq_copy(i, 2).start()

    stat_copy().wait_recv()

    @pl.when(m <= 1)
    def _():
        pl.semaphore_wait(ready, 2 - m)
        xl_copy(0).start()

    @pl.when(m == 0)
    def _():
        xl_copy(1).start()

    @pl.loop(0, 2)
    def _(i):
        share(i)

    @pl.loop(0, 2)
    def _(i):
        hand_on(i)

    key_at = lax.broadcasted_iota(jnp.int32, (half, half), 0)
    query_at = lax.broadcasted_iota(jnp.int32, (half, half), 1)
    causal = key_at <= query_at

    def flat(x):
        return x.reshape(-1, dim)

    def tile(kk, vv, qq, gg, lse, delta):
        scores = dot(kk, qq, NT) * (scale * log2e) - lse
        return jnp.exp2(scores), dot(vv, gg, NT) - delta

    def compute(i):
        keys = [halo[i, :, :, 0], kv_buf[i, 0:2, 0], kv_buf[i, 4:6, 0]]
        vals = [halo[i, :, :, 1], kv_buf[i, 0:2, 1], kv_buf[i, 4:6, 1]]
        keys = jnp.concatenate([flat(x) for x in keys], axis=0)
        vals = jnp.concatenate([flat(x) for x in vals], axis=0)
        at = pl.ds(4 * lo + i, 1)
        parts = []
        for b in range(2):
            kk, vv = keys[b * half : (b + 4) * half], vals[b * half : (b + 4) * half]
            k2, v2 = flat(kv_buf[i, 4 * b + 2 : 4 * b + 4, 0]), flat(kv_buf[i, 4 * b + 2 : 4 * b + 4, 1])
            qq, gg = flat(qg_buf[i, 4 * b : 4 * b + 4, 0]), flat(qg_buf[i, 4 * b : 4 * b + 4, 1])
            lse, delta = stats[b, 0, at, :], stats[b, 1, at, :]
            probs, pgrad = tile(kk, vv, qq, gg, lse, delta)
            own = probs[3 * half :]
            own = jnp.concatenate([jnp.where(causal, own[:, :half], 0.0), own[:, half:]], axis=1)
            probs = jnp.concatenate([probs[: 3 * half], own], axis=0)
            sgrad = (probs * pgrad).astype(BF16)
            dv = dot(probs.astype(BF16), gg, NN)
            dk = dot(sgrad, qq, NN) * scale
            q2, g2 = qq[half:], gg[half:]
            probs, pgrad = tile(k2, v2, q2, g2, lse[:, half:], delta[:, half:])
            probs = jnp.where(causal, probs, 0.0)
            sgrad2 = (probs * pgrad).astype(BF16)
            acc[i, b, 1, 1] += dot(probs.astype(BF16), g2, NN)
            acc[i, b, 1, 0] += dot(sgrad2, q2, NN) * scale
            dq = dot(sgrad, kk, TN)
            dq = jnp.concatenate([dq[:half], dq[half:] + dot(sgrad2, k2, TN)], axis=0) * scale
            dq_buf[i, 4 * b : 4 * b + 4] = dq.astype(BF16).reshape(4, rows, dim)
            parts.append((dk, dv))
        for which in range(2):
            e, o = parts[0][which], parts[1][which]
            halo_grad[i, 0, which] = e[:half].astype(BF16)
            halo_grad[i, 1, which] = (e[half : 2 * half] + o[:half]).astype(BF16)
            chain[i, which] = e[2 * half : 3 * half] + o[half : 2 * half]
            acc[i, 0, 0, which] += e[3 * half :] + o[2 * half : 3 * half]
            acc[i, 1, 0, which] += o[3 * half :]

    def wrapped(i, slot, b, first):
        kk, vv = flat(kv_buf[i, 4 * b : 4 * b + 4, 0]), flat(kv_buf[i, 4 * b : 4 * b + 4, 1])
        qq, gg = flat(xq[i, slot, :, 0]), flat(xq[i, slot, :, 1])
        at = pl.ds(4 * lo + i, 1)
        lse = xl[slot // 2, slot % 2, 0, at, :][:, half:]
        delta = xl[slot // 2, slot % 2, 1, at, :][:, half:]
        probs, pgrad = tile(kk, vv, qq, gg, lse, delta)
        sgrad = (probs * pgrad).astype(BF16)
        dv = dot(probs.astype(BF16), gg, NN)
        dk = dot(sgrad, qq, NN) * scale
        for part in range(2):
            cut = slice(part * half, (part + 1) * half)
            acc[i, b, part, 0] += dk[cut]
            acc[i, b, part, 1] += dv[cut]
        dq = dot(sgrad, kk, TN) * scale
        if first:
            xacc[slot] = dq
        else:
            xacc[slot] += dq

    def send_dq(i):
        for p in peers:
            dq_copy(i, *p).start()

    def pass_back(i):
        @pl.when(m >= 1)
        def _():
            @pl.when(m <= last - 1)
            def _():
                back_copy(i, 0).wait_recv()

            halo_grad[i, 2] = (chain[i] + halo_in[i, 0].astype(F32)).astype(BF16)
            back_copy(i, 2).start()

    def wrapped_last(i):
        @pl.when(m == last)
        def _():
            for slot in range(3):
                xq_arrived(i, slot).wait_recv()
            for slot in range(2):
                wrapped(i, slot, 0, True)
            wrapped(i, 2, 1, True)
            for slot in range(2):
                wrapped(i, slot, 1, False)
            xdq[i] = xacc[...].astype(BF16)
            for n in range(3):
                xd_copy(i, n).start()

    def wrapped_one(i):
        @pl.when(m == last - 1)
        def _():
            xq_arrived(i, 0).wait_recv()
            wrapped(i, 0, 1, True)
            xdq[i, 0] = xacc[0].astype(BF16)
            xd_copy(i, 2).start()

    def finish(i):
        @pl.when(m <= last - 1)
        def _():
            back_copy(i, 1).wait_recv()
            back_copy(i, 2).wait_recv()

        for which in range(2):
            for b in range(2):
                first = acc[i, b, 0, which] + halo_in[i, 1 + b, which].astype(F32)
                dkv_buf[i, 4 * b : 4 * b + 2, which] = first.astype(BF16).reshape(2, rows, dim)
                second = acc[i, b, 1, which]
                dkv_buf[i, 4 * b + 2 : 4 * b + 4, which] = second.astype(BF16).reshape(2, rows, dim)
        for p in peers:
            dkv_copy(i, *p).start()

    def finish_first(i):
        xd_copy(i, 2).wait_recv()
        more = xd_in[i, 2].astype(F32).reshape(2, rows, dim)
        dq_buf[i, 2:4] = (dq_buf[i, 2:4].astype(F32) + more).astype(BF16)

        @pl.when(m == 0)
        def _():
            for slot in range(2):
                xd_copy(i, slot).wait_recv()
                at = slice(4 * slot + 2, 4 * slot + 4)
                more = xd_in[i, slot].astype(F32).reshape(2, rows, dim)
                dq_buf[i, at] = (dq_buf[i, at].astype(F32) + more).astype(BF16)

        send_dq(i)

    @pl.when(m == last)
    def _():
        xl_arrived(0).wait_recv()
        xl_arrived(1).wait_recv()

    @pl.when(m == last - 1)
    def _():
        xl_arrived(0).wait_recv()

    def grads(i):
        split_arrived(1, i, 0)
        @pl.when(m >= 2)
        def _():
            halo_copy(i, 0).wait_recv()

        @pl.when(m >= 1)
        def _():
            halo_copy(i, 1).wait_recv()

        compute(i)

        @pl.when(m >= 2)
        def _():
            back_copy(i, 0).start()

        @pl.when(m >= 1)
        def _():
            back_copy(i, 1).start()

        @pl.when(m >= 2)
        def _():
            send_dq(i)

    @pl.loop(0, hpg)
    def _(i):
        split_arrived(0, i, 1)
        wrapped_last(i)
        grads(i)

        @pl.when((i >= 1) & (i + 1 < hpg))
        def _():
            hand_on(i + 1)

        @pl.when(i >= 1)
        def _():
            pass_back(i - 1)

        @pl.when(i + 2 < hpg)
        def _():
            share(i + 2)

        @pl.when(i >= 1)
        def _():
            wrapped_one(i - 1)

    wrapped_one(hpg - 1)

    @pl.loop(0, hpg)
    def _(i):
        finish(i)

        @pl.when(i == 1)
        def _():
            pass_back(hpg - 1)

        @pl.when((m <= 1) & (i >= 2))
        def _():
            finish_first(i - 2)

    @pl.when(m <= 1)
    def _():
        @pl.loop(hpg - 2, hpg)
        def _(i):
            finish_first(i)

    @pl.loop(0, hpg)
    def _(i):
        own_dq, own_dkv = keep(i)
        own_dq.start()
        own_dkv.start()

    @pl.loop(0, hpg)
    def _(i):
        for p in peers:
            dq_copy(i, *p).wait_recv()
            dkv_copy(i, *p).wait_recv()
        own_dq, own_dkv = keep(i)
        own_dq.wait()
        own_dkv.wait()

    stat_copy().wait_send()

    @pl.loop(0, hpg)
    def _(i):
        for p in peers:
            for kind in range(2):
                split_copy(kind, i, *p).wait_send()
            dq_copy(i, *p).wait_send()
            dkv_copy(i, *p).wait_send()

        @pl.when(m <= last - 1)
        def _():
            halo_copy(i, 1).wait_send()
            halo_copy(i, 2).wait_send()

            @pl.when(m >= 1)
            def _():
                halo_copy(i, 0).wait_send()

        @pl.when(m >= 2)
        def _():
            back_copy(i, 0).wait_send()

        @pl.when(m >= 1)
        def _():
            back_copy(i, 1).wait_send()
            back_copy(i, 2).wait_send()

        @pl.when(m == 0)
        def _():
            xq_copy(i, 0).wait_send()
            xq_copy(i, 1).wait_send()

        @pl.when(m <= 1)
        def _():
            xq_copy(i, 2).wait_send()

        @pl.when(m >= last - 1)
        def _():
            xd_copy(i, 2).wait_send()

        @pl.when(m == last)
        def _():
            xd_copy(i, 0).wait_send()
            xd_copy(i, 1).wait_send()

    @pl.when(m <= 1)
    def _():
        xl_copy(0).wait_send()

    @pl.when(m == 0)
    def _():
        xl_copy(1).wait_send()


PARTS = 2


def join_heads(dq_ref, dkv_ref, dq_out, dk_out, dv_out, by_head, by_row, s_load, s_store):
    groups, hpg, rows, dim = dq_ref.shape
    size = rows // PARTS
    loads, stores = [], []
    for n, src in enumerate((dq_ref, dkv_ref.at[:, :, 0], dkv_ref.at[:, :, 1])):
        for part in range(PARTS):
            cut = pl.ds(part * size, size)
            loads.append(pltpu.make_async_copy(src.at[:, :, cut], by_head.at[n, :, :, cut], s_load.at[n, part]))
            loads[-1].start()
    for n, dst in enumerate((dq_out, dk_out, dv_out)):
        for part in range(PARTS):
            cut = pl.ds(part * size, size)
            loads[n * PARTS + part].wait()
            block = by_head[n, :, :, part * size : (part + 1) * size].reshape(groups * hpg, size, dim)
            by_row[n, part * size : (part + 1) * size] = jnp.swapaxes(block, 0, 1)
            stores.append(pltpu.make_async_copy(by_row.at[n, cut], dst.at[cut], s_store.at[n, part]))
            stores[-1].start()
    for store in stores:
        store.wait()


def on_device(queries, key_vectors, value_vectors, grad_output, logsumexp, row_delta):
    rows, heads, dim = queries.shape
    hpg = heads // GROUP
    half = 2 * rows
    rows_total = lax.axis_size("seq") // 2
    hbm = pl.BlockSpec(memory_space=pl.ANY)
    dma = pltpu.SemaphoreType.DMA
    dq_shape = jax.ShapeDtypeStruct((GROUP, hpg, rows, dim), BF16)
    dkv_shape = jax.ShapeDtypeStruct((GROUP, hpg, 2, rows, dim), BF16)

    def body(*refs):
        kernel(rows_total, *refs)

    dq, dkv = pl.pallas_call(
        body,
        out_shape=(dq_shape, dkv_shape),
        in_specs=[hbm] * 6,
        out_specs=(hbm, hbm),
        scratch_shapes=[
            pltpu.VMEM((2, GROUP, hpg, 2, rows, dim), BF16),
            pltpu.VMEM((2, hpg, GROUP, 2, rows, dim), BF16),
            pltpu.VMEM((2, 2, *logsumexp.shape), F32),
            pltpu.VMEM((hpg, 3, 2, 2, rows, dim), BF16),
            pltpu.VMEM((hpg, 3, 2, half, dim), BF16),
            pltpu.VMEM((hpg, 3, 2, half, dim), BF16),
            pltpu.VMEM((hpg, 2, 2, 2, half, dim), F32),
            pltpu.VMEM((hpg, GROUP, rows, dim), BF16),
            pltpu.VMEM((hpg, GROUP, 2, rows, dim), BF16),
            pltpu.VMEM((hpg, 3, 2, 2, rows, dim), BF16),
            pltpu.VMEM((2, 2, 2, *logsumexp.shape), F32),
            pltpu.VMEM((3, half, dim), F32),
            pltpu.VMEM((hpg, 3, half, dim), BF16),
            pltpu.VMEM((hpg, 3, half, dim), BF16),
            pltpu.VMEM((hpg, 2, half, dim), F32),
            pltpu.VMEM((4, rows, heads, dim), BF16),
            pltpu.VMEM((2, *logsumexp.shape), F32),
            pltpu.SemaphoreType.REGULAR,
            dma((6,)),
            dma((hpg, 2)),
            *[dma((2, hpg, GROUP - 1))] * 2,
            *[dma((1,))] * 2,
            *[dma((hpg, 3))] * 4,
            *[dma((hpg, GROUP - 1))] * 4,
            *[dma((hpg, 3))] * 2,
            *[dma((2,))] * 2,
            *[dma((hpg, 3))] * 2,
        ],
        compiler_params=pltpu.CompilerParams(
            collective_id=0, has_side_effects=True, vmem_limit_bytes=60 << 20
        ),
        name="window_grads",
    )(queries, key_vectors, value_vectors, grad_output, logsumexp, row_delta)

    out = jax.ShapeDtypeStruct((rows, heads, dim), BF16)
    return pl.pallas_call(
        join_heads,
        out_shape=(out, out, out),
        in_specs=[hbm] * 2,
        out_specs=(hbm, hbm, hbm),
        scratch_shapes=[
            pltpu.VMEM((3, GROUP, hpg, rows, dim), BF16),
            pltpu.VMEM((3, rows, heads, dim), BF16),
            dma((3, PARTS)),
            dma((3, PARTS)),
        ],
        compiler_params=pltpu.CompilerParams(vmem_limit_bytes=60 << 20),
        name="join_heads",
    )(dq, dkv)


def solution(mesh):
    rows = P(("seq", "head"), None, None)
    stats = P("head", "seq")
    return jax.shard_map(
        on_device,
        mesh=mesh,
        in_specs=(rows, rows, rows, rows, stats, stats),
        out_specs=(rows, rows, rows),
        check_vma=False,
    )
```

```python
import math

import jax
import jax.numpy as jnp
from jax import lax
from jax.experimental import pallas as pl
from jax.experimental.pallas import tpu as pltpu
from jax.sharding import PartitionSpec as P

MESH = pl.DeviceIdType.MESH
GROUP = 8
BF16, F32 = jnp.bfloat16, jnp.float32
NT = (((1,), (1,)), ((), ()))
NN = (((1,), (0,)), ((), ()))
TN = (((0,), (0,)), ((), ()))


def dot(a, b, dims):
    return lax.dot_general(a, b, dims, preferred_element_type=F32)


def kernel(
    rows_total, q_ref, k_ref, v_ref, g_ref, lse_ref, delta_ref, fin_dq, fin_dkv,
    sent, got, stats, halo, halo_grad, halo_in, acc,
    dq_buf, dkv_buf, xq, xl, xacc, xdq, xd_in, chain, local, local_stats, ready, s_in, s_own,
    s_split, r_split, s_st, r_st, s_hf, r_hf, s_hb, r_hb,
    s_dq, r_dq, s_dkv, r_dkv, s_xq, r_xq, s_xl, r_xl, s_xd, r_xd,
):
    rows, heads, dim = q_ref.shape
    hpg = heads // GROUP
    half = 2 * rows
    last = rows_total - 1
    scale = dim ** -0.5
    log2e = math.log2(math.e)

    s, h = lax.axis_index("seq"), lax.axis_index("head")
    lo, m = s % 2, s // 2
    hi, core = h // 2, h % 2
    place = lo * 4 + hi * 2 + core
    mine = hi * 4 + core * 2 + lo

    def peer(o):
        lo2, hi2, core2 = (lo + o % 2) % 2, (hi + o // 2 % 2) % 2, (core + o // 4) % 2
        return (2 * m + lo2, hi2 * 2 + core2), lo2 * 4 + hi2 * 2 + core2, hi2 * 4 + core2 * 2 + lo2

    peers = [(o, *peer(o)) for o in (2, 3, 1, 6, 7, 5, 4)]

    def row(step):
        return (2 * ((m + step + rows_total) % rows_total) + lo, h)

    def copy(src, dst, send, recv, to):
        return pltpu.make_async_remote_copy(
            src_ref=src, dst_ref=dst, send_sem=send, recv_sem=recv, device_id=to, device_id_type=MESH
        )

    kv_buf, qg_buf = got.at[0], got.at[1]

    def split_copy(kind, i, o, to, place2, mine2):
        return copy(
            sent.at[kind, mine2, i], got.at[kind, i, place], s_split.at[kind, i, o - 1], r_split.at[kind, i, o - 1], to
        )

    def split_arrived(kind, i, part):
        @pl.when(hi == part)
        def _():
            for p in peers:
                if p[0] in (1, 4, 5):
                    split_copy(kind, i, *p).wait_recv()

        @pl.when(hi != part)
        def _():
            for p in peers:
                if p[0] not in (1, 4, 5):
                    split_copy(kind, i, *p).wait_recv()

    def dq_copy(i, o, to, place2, mine2):
        return copy(dq_buf.at[i, place2], fin_dq.at[mine, i], s_dq.at[i, o - 1], r_dq.at[i, o - 1], to)

    def dkv_copy(i, o, to, place2, mine2):
        return copy(dkv_buf.at[i, place2], fin_dkv.at[mine, i], s_dkv.at[i, o - 1], r_dkv.at[i, o - 1], to)

    def keep(i):
        return (
            pltpu.make_async_copy(dq_buf.at[i, place], fin_dq.at[mine, i], s_own.at[i, 0]),
            pltpu.make_async_copy(dkv_buf.at[i, place], fin_dkv.at[mine, i], s_own.at[i, 1]),
        )

    def stat_copy():
        return copy(stats.at[lo], stats.at[lo], s_st.at[0], r_st.at[0], peer(1)[0])

    def halo_copy(i, n):
        src = halo.at[i, 2] if n == 0 else kv_buf.at[i, pl.ds((0, 4)[n - 1], 2)]
        return copy(src, halo.at[i, n], s_hf.at[i, n], r_hf.at[i, n], row(1))

    def back_copy(i, n):
        return copy(halo_grad.at[i, n], halo_in.at[i, n], s_hb.at[i, n], r_hb.at[i, n], row(-1))

    def xq_copy(i, n):
        second_half = qg_buf.at[i, pl.ds((2, 6, 2)[n], 2)]
        slot = (0, 1, 2 * (m % 2))[n]
        return copy(second_half, xq.at[i, slot], s_xq.at[i, n], r_xq.at[i, slot], row((-1, -1, -2)[n]))

    def xq_arrived(i, slot):
        to = xq.at[i, slot]
        return copy(to, to, s_xq.at[i, 0], r_xq.at[i, slot], row(1))

    def xl_copy(n):
        slot = (m % 2, 0)[n]
        return copy(stats, xl.at[slot], s_xl.at[n], r_xl.at[slot], row((-2, -1)[n]))

    def xl_arrived(slot):
        return copy(xl.at[slot], xl.at[slot], s_xl.at[0], r_xl.at[slot], row(1))

    def xd_copy(i, n):
        slot = (0, 1, 2 * ((m - (rows_total - 2)) % 2))[n]
        return copy(xdq.at[i, slot], xd_in.at[i, n], s_xd.at[i, n], r_xd.at[i, n], row((1, 1, 2)[n]))

    def load_of(n, src=k_ref):
        return pltpu.make_async_copy(src, local.at[n], s_in.at[n])

    stat_loads = [
        pltpu.make_async_copy(src, local_stats.at[n], s_in.at[4 + n]) for n, src in enumerate((lse_ref, delta_ref))
    ]
    for n, src in enumerate((k_ref, v_ref, q_ref, g_ref)):
        load_of(n, src).start()
    for load in stat_loads:
        load.start()

    barrier = pltpu.get_barrier_semaphore()
    for _, to, _, _ in peers:
        pl.semaphore_signal(barrier, inc=1, device_id=to, device_id_type=MESH)

    def tell(sem, step):
        pl.semaphore_signal(sem, inc=1, device_id=row(step), device_id_type=MESH)

    @pl.when(m <= last - 1)
    def _():
        tell(barrier, 1)

    @pl.when(m >= 1)
    def _():
        tell(barrier, -1)

    @pl.when(m <= 1)
    def _():
        tell(barrier, -2)

    @pl.when(m == 0)
    def _():
        tell(barrier, -1)

    def split_heads(kind):
        for which in range(2):
            load_of(2 * kind + which).wait()
            by_head = jnp.swapaxes(local[2 * kind + which], 0, 1)
            sent[kind, :, :, which] = by_head.reshape(GROUP, hpg, rows, dim)
        got[kind, :, pl.ds(place, 1)] = sent[kind, mine][:, None]

    first, second = hi, 1 - hi
    split_heads(first)
    for load in stat_loads:
        load.wait()
    stats[lo, 0] = local_stats[0] * log2e
    stats[lo, 1] = local_stats[1]

    one, none = jnp.int32(1), jnp.int32(0)
    along = jnp.where(m >= 1, one, none) + jnp.where(m <= last - 1, one, none)
    ends = jnp.where(m >= last - 1, one, none) + jnp.where(m == last, one, none)
    pl.semaphore_wait(barrier, GROUP - 1 + along + ends)

    @pl.when(m >= last - 1)
    def _():
        tell(ready, 2)

    @pl.when(m == last)
    def _():
        tell(ready, 1)

    stat_copy().start()

    def send(kind, i):
        for p in peers:
            split_copy(kind, i, *p).start()

    @pl.loop(0, 2)
    def _(i):
        send(first, i)

    split_heads(second)

    @pl.loop(0, hpg - 2)
    def _(i):
        send(second, i)
        send(first, i + 2)

    @pl.loop(hpg - 2, hpg)
    def _(i):
        send(second, i)

    acc[...] = jnp.zeros_like(acc)

    @pl.when(m <= 1)
    def _():
        halo[:, 0] = jnp.zeros_like(halo[:, 0])

    @pl.when(m == 0)
    def _():
        halo[:, 1:3] = jnp.zeros_like(halo[:, 1:3])

    @pl.when(m == last)
    def _():
        halo_in[...] = jnp.zeros_like(halo_in)

    def hand_on(i):
        @pl.when(m >= 1)
        def _():
            halo_copy(i, 2).wait_recv()

            @pl.when(m <= last - 1)
            def _():
                halo_copy(i, 0).start()

    def share_keys(i):
        split_arrived(0, i, 0)

        @pl.when(m <= last - 1)
        def _():
            halo_copy(i, 2).start()
            halo_copy(i, 1).start()

    def share_queries(i):
        split_arrived(1, i, 1)

        @pl.when(m == 0)
        def _():
            xq_copy(i, 0).start()
            xq_copy(i, 1).start()

        @pl.when(m == 1)
        def _():
            xq_copy(i, 2).start()

        @pl.when((m == 0) & (i >= 1))
        def _():
            xq_copy(i - 1, 2).start()

        @pl.when((m == 0) & (i == hpg - 1))
        def _():
            xq_copy(i, 2).start()

    @pl.loop(0, 2)
    def _(i):
        share_keys(i)

    stat_copy().wait_recv()

    @pl.when(m <= 1)
    def _():
        pl.semaphore_wait(ready, 2 - m)
        xl_copy(0).start()

    @pl.when(m == 0)
    def _():
        xl_copy(1).start()

    @pl.loop(0, 2)
    def _(i):
        share_queries(i)

    @pl.loop(0, 2)
    def _(i):
        hand_on(i)

    key_at = lax.broadcasted_iota(jnp.int32, (half, half), 0)
    query_at = lax.broadcasted_iota(jnp.int32, (half, half), 1)
    causal = key_at <= query_at

    def flat(x):
        return x.reshape(-1, dim)

    def tile(kk, vv, qq, gg, lse, delta):
        scores = dot(kk, qq, NT) * (scale * log2e) - lse
        return jnp.exp2(scores), dot(vv, gg, NT) - delta

    def compute(i):
        keys = [halo[i, :, :, 0], kv_buf[i, 0:2, 0], kv_buf[i, 4:6, 0]]
        vals = [halo[i, :, :, 1], kv_buf[i, 0:2, 1], kv_buf[i, 4:6, 1]]
        keys = jnp.concatenate([flat(x) for x in keys], axis=0)
        vals = jnp.concatenate([flat(x) for x in vals], axis=0)
        at = pl.ds(4 * lo + i, 1)
        parts = []
        for b in range(2):
            kk, vv = keys[b * half : (b + 4) * half], vals[b * half : (b + 4) * half]
            k2, v2 = flat(kv_buf[i, 4 * b + 2 : 4 * b + 4, 0]), flat(kv_buf[i, 4 * b + 2 : 4 * b + 4, 1])
            qq, gg = flat(qg_buf[i, 4 * b : 4 * b + 4, 0]), flat(qg_buf[i, 4 * b : 4 * b + 4, 1])
            lse, delta = stats[b, 0, at, :], stats[b, 1, at, :]
            probs, pgrad = tile(kk, vv, qq, gg, lse, delta)
            own = probs[3 * half :]
            own = jnp.concatenate([jnp.where(causal, own[:, :half], 0.0), own[:, half:]], axis=1)
            probs = jnp.concatenate([probs[: 3 * half], own], axis=0)
            sgrad = (probs * pgrad).astype(BF16)
            dv = dot(probs.astype(BF16), gg, NN)
            dk = dot(sgrad, qq, NN) * scale
            q2, g2 = qq[half:], gg[half:]
            probs, pgrad = tile(k2, v2, q2, g2, lse[:, half:], delta[:, half:])
            probs = jnp.where(causal, probs, 0.0)
            sgrad2 = (probs * pgrad).astype(BF16)
            acc[i, b, 1, 1] += dot(probs.astype(BF16), g2, NN)
            acc[i, b, 1, 0] += dot(sgrad2, q2, NN) * scale
            dq = dot(sgrad, kk, TN)
            dq = jnp.concatenate([dq[:half], dq[half:] + dot(sgrad2, k2, TN)], axis=0) * scale
            dq_buf[i, 4 * b : 4 * b + 4] = dq.astype(BF16).reshape(4, rows, dim)
            parts.append((dk, dv))
        for which in range(2):
            e, o = parts[0][which], parts[1][which]
            halo_grad[i, 0, which] = e[:half].astype(BF16)
            halo_grad[i, 1, which] = (e[half : 2 * half] + o[:half]).astype(BF16)
            chain[i, which] = e[2 * half : 3 * half] + o[half : 2 * half]
            acc[i, 0, 0, which] += e[3 * half :] + o[2 * half : 3 * half]
            acc[i, 1, 0, which] += o[3 * half :]

    def wrapped(i, slot, b, first):
        kk, vv = flat(kv_buf[i, 4 * b : 4 * b + 4, 0]), flat(kv_buf[i, 4 * b : 4 * b + 4, 1])
        qq, gg = flat(xq[i, slot, :, 0]), flat(xq[i, slot, :, 1])
        at = pl.ds(4 * lo + i, 1)
        lse = xl[slot // 2, slot % 2, 0, at, :][:, half:]
        delta = xl[slot // 2, slot % 2, 1, at, :][:, half:]
        probs, pgrad = tile(kk, vv, qq, gg, lse, delta)
        sgrad = (probs * pgrad).astype(BF16)
        dv = dot(probs.astype(BF16), gg, NN)
        dk = dot(sgrad, qq, NN) * scale
        for part in range(2):
            cut = slice(part * half, (part + 1) * half)
            acc[i, b, part, 0] += dk[cut]
            acc[i, b, part, 1] += dv[cut]
        dq = dot(sgrad, kk, TN) * scale
        if first:
            xacc[slot] = dq
        else:
            xacc[slot] += dq

    def send_dq(i):
        for p in peers:
            dq_copy(i, *p).start()

    def pass_back(i):
        @pl.when(m >= 1)
        def _():
            @pl.when(m <= last - 1)
            def _():
                back_copy(i, 0).wait_recv()

            halo_grad[i, 2] = (chain[i] + halo_in[i, 0].astype(F32)).astype(BF16)
            back_copy(i, 2).start()

    def wrapped_last(i):
        @pl.when(m == last)
        def _():
            for slot in range(3):
                xq_arrived(i, slot).wait_recv()
            for slot in range(2):
                wrapped(i, slot, 0, True)
            wrapped(i, 2, 1, True)
            for slot in range(2):
                wrapped(i, slot, 1, False)
            xdq[i] = xacc[...].astype(BF16)
            for n in range(3):
                xd_copy(i, n).start()

    def wrapped_one(i):
        @pl.when(m == last - 1)
        def _():
            xq_arrived(i, 0).wait_recv()
            wrapped(i, 0, 1, True)
            xdq[i, 0] = xacc[0].astype(BF16)
            xd_copy(i, 2).start()

    def finish(i):
        @pl.when(m <= last - 1)
        def _():
            back_copy(i, 1).wait_recv()
            back_copy(i, 2).wait_recv()

        for which in range(2):
            for b in range(2):
                first = acc[i, b, 0, which] + halo_in[i, 1 + b, which].astype(F32)
                dkv_buf[i, 4 * b : 4 * b + 2, which] = first.astype(BF16).reshape(2, rows, dim)
                second = acc[i, b, 1, which]
                dkv_buf[i, 4 * b + 2 : 4 * b + 4, which] = second.astype(BF16).reshape(2, rows, dim)
        for p in peers:
            dkv_copy(i, *p).start()

    def finish_first(i):
        xd_copy(i, 2).wait_recv()
        more = xd_in[i, 2].astype(F32).reshape(2, rows, dim)
        dq_buf[i, 2:4] = (dq_buf[i, 2:4].astype(F32) + more).astype(BF16)

        @pl.when(m == 0)
        def _():
            for slot in range(2):
                xd_copy(i, slot).wait_recv()
                at = slice(4 * slot + 2, 4 * slot + 4)
                more = xd_in[i, slot].astype(F32).reshape(2, rows, dim)
                dq_buf[i, at] = (dq_buf[i, at].astype(F32) + more).astype(BF16)

        send_dq(i)

    @pl.when(m == last)
    def _():
        xl_arrived(0).wait_recv()
        xl_arrived(1).wait_recv()

    @pl.when(m == last - 1)
    def _():
        xl_arrived(0).wait_recv()

    def grads(i):
        split_arrived(1, i, 0)
        @pl.when(m >= 2)
        def _():
            halo_copy(i, 0).wait_recv()

        @pl.when(m >= 1)
        def _():
            halo_copy(i, 1).wait_recv()

        compute(i)

        @pl.when(m >= 2)
        def _():
            back_copy(i, 0).start()

        @pl.when(m >= 1)
        def _():
            back_copy(i, 1).start()

        @pl.when(m >= 2)
        def _():
            send_dq(i)

    @pl.loop(0, hpg)
    def _(i):
        split_arrived(0, i, 1)
        wrapped_last(i)
        grads(i)

        @pl.when((i >= 1) & (i + 1 < hpg))
        def _():
            hand_on(i + 1)

        @pl.when(i >= 1)
        def _():
            pass_back(i - 1)

        @pl.when(i + 2 < hpg)
        def _():
            share_keys(i + 2)
            share_queries(i + 2)

        @pl.when(i >= 1)
        def _():
            wrapped_one(i - 1)

    wrapped_one(hpg - 1)

    @pl.loop(0, hpg)
    def _(i):
        finish(i)

        @pl.when(i == 1)
        def _():
            pass_back(hpg - 1)

        @pl.when((m <= 1) & (i >= 2))
        def _():
            finish_first(i - 2)

    @pl.when(m <= 1)
    def _():
        @pl.loop(hpg - 2, hpg)
        def _(i):
            finish_first(i)

    @pl.loop(0, hpg)
    def _(i):
        own_dq, own_dkv = keep(i)
        own_dq.start()
        own_dkv.start()

    @pl.loop(0, hpg)
    def _(i):
        for p in peers:
            dq_copy(i, *p).wait_recv()
            dkv_copy(i, *p).wait_recv()
        own_dq, own_dkv = keep(i)
        own_dq.wait()
        own_dkv.wait()

    stat_copy().wait_send()

    @pl.loop(0, hpg)
    def _(i):
        for p in peers:
            for kind in range(2):
                split_copy(kind, i, *p).wait_send()
            dq_copy(i, *p).wait_send()
            dkv_copy(i, *p).wait_send()

        @pl.when(m <= last - 1)
        def _():
            halo_copy(i, 1).wait_send()
            halo_copy(i, 2).wait_send()

            @pl.when(m >= 1)
            def _():
                halo_copy(i, 0).wait_send()

        @pl.when(m >= 2)
        def _():
            back_copy(i, 0).wait_send()

        @pl.when(m >= 1)
        def _():
            back_copy(i, 1).wait_send()
            back_copy(i, 2).wait_send()

        @pl.when(m == 0)
        def _():
            xq_copy(i, 0).wait_send()
            xq_copy(i, 1).wait_send()

        @pl.when(m <= 1)
        def _():
            xq_copy(i, 2).wait_send()

        @pl.when(m >= last - 1)
        def _():
            xd_copy(i, 2).wait_send()

        @pl.when(m == last)
        def _():
            xd_copy(i, 0).wait_send()
            xd_copy(i, 1).wait_send()

    @pl.when(m <= 1)
    def _():
        xl_copy(0).wait_send()

    @pl.when(m == 0)
    def _():
        xl_copy(1).wait_send()


PARTS = 2


def join_heads(dq_ref, dkv_ref, dq_out, dk_out, dv_out, by_head, by_row, s_load, s_store):
    groups, hpg, rows, dim = dq_ref.shape
    size = rows // PARTS
    loads, stores = [], []
    for n, src in enumerate((dq_ref, dkv_ref.at[:, :, 0], dkv_ref.at[:, :, 1])):
        for part in range(PARTS):
            cut = pl.ds(part * size, size)
            loads.append(pltpu.make_async_copy(src.at[:, :, cut], by_head.at[n, :, :, cut], s_load.at[n, part]))
            loads[-1].start()
    for n, dst in enumerate((dq_out, dk_out, dv_out)):
        for part in range(PARTS):
            cut = pl.ds(part * size, size)
            loads[n * PARTS + part].wait()
            block = by_head[n, :, :, part * size : (part + 1) * size].reshape(groups * hpg, size, dim)
            by_row[n, part * size : (part + 1) * size] = jnp.swapaxes(block, 0, 1)
            stores.append(pltpu.make_async_copy(by_row.at[n, cut], dst.at[cut], s_store.at[n, part]))
            stores[-1].start()
    for store in stores:
        store.wait()


def on_device(queries, key_vectors, value_vectors, grad_output, logsumexp, row_delta):
    rows, heads, dim = queries.shape
    hpg = heads // GROUP
    half = 2 * rows
    rows_total = lax.axis_size("seq") // 2
    hbm = pl.BlockSpec(memory_space=pl.ANY)
    dma = pltpu.SemaphoreType.DMA
    dq_shape = jax.ShapeDtypeStruct((GROUP, hpg, rows, dim), BF16)
    dkv_shape = jax.ShapeDtypeStruct((GROUP, hpg, 2, rows, dim), BF16)

    def body(*refs):
        kernel(rows_total, *refs)

    dq, dkv = pl.pallas_call(
        body,
        out_shape=(dq_shape, dkv_shape),
        in_specs=[hbm] * 6,
        out_specs=(hbm, hbm),
        scratch_shapes=[
            pltpu.VMEM((2, GROUP, hpg, 2, rows, dim), BF16),
            pltpu.VMEM((2, hpg, GROUP, 2, rows, dim), BF16),
            pltpu.VMEM((2, 2, *logsumexp.shape), F32),
            pltpu.VMEM((hpg, 3, 2, 2, rows, dim), BF16),
            pltpu.VMEM((hpg, 3, 2, half, dim), BF16),
            pltpu.VMEM((hpg, 3, 2, half, dim), BF16),
            pltpu.VMEM((hpg, 2, 2, 2, half, dim), F32),
            pltpu.VMEM((hpg, GROUP, rows, dim), BF16),
            pltpu.VMEM((hpg, GROUP, 2, rows, dim), BF16),
            pltpu.VMEM((hpg, 3, 2, 2, rows, dim), BF16),
            pltpu.VMEM((2, 2, 2, *logsumexp.shape), F32),
            pltpu.VMEM((3, half, dim), F32),
            pltpu.VMEM((hpg, 3, half, dim), BF16),
            pltpu.VMEM((hpg, 3, half, dim), BF16),
            pltpu.VMEM((hpg, 2, half, dim), F32),
            pltpu.VMEM((4, rows, heads, dim), BF16),
            pltpu.VMEM((2, *logsumexp.shape), F32),
            pltpu.SemaphoreType.REGULAR,
            dma((6,)),
            dma((hpg, 2)),
            *[dma((2, hpg, GROUP - 1))] * 2,
            *[dma((1,))] * 2,
            *[dma((hpg, 3))] * 4,
            *[dma((hpg, GROUP - 1))] * 4,
            *[dma((hpg, 3))] * 2,
            *[dma((2,))] * 2,
            *[dma((hpg, 3))] * 2,
        ],
        compiler_params=pltpu.CompilerParams(
            collective_id=0, has_side_effects=True, vmem_limit_bytes=60 << 20
        ),
        name="window_grads",
    )(queries, key_vectors, value_vectors, grad_output, logsumexp, row_delta)

    out = jax.ShapeDtypeStruct((rows, heads, dim), BF16)
    return pl.pallas_call(
        join_heads,
        out_shape=(out, out, out),
        in_specs=[hbm] * 2,
        out_specs=(hbm, hbm, hbm),
        scratch_shapes=[
            pltpu.VMEM((3, GROUP, hpg, rows, dim), BF16),
            pltpu.VMEM((3, rows, heads, dim), BF16),
            dma((3, PARTS)),
            dma((3, PARTS)),
        ],
        compiler_params=pltpu.CompilerParams(vmem_limit_bytes=60 << 20),
        name="join_heads",
    )(dq, dkv)


def solution(mesh):
    rows = P(("seq", "head"), None, None)
    stats = P("head", "seq")
    return jax.shard_map(
        on_device,
        mesh=mesh,
        in_specs=(rows, rows, rows, rows, stats, stats),
        out_specs=(rows, rows, rows),
        check_vma=False,
    )
```

```python
import math

import jax
import jax.numpy as jnp
from jax import lax
from jax.experimental import pallas as pl
from jax.experimental.pallas import tpu as pltpu
from jax.sharding import PartitionSpec as P

MESH = pl.DeviceIdType.MESH
GROUP = 8
BF16, F32 = jnp.bfloat16, jnp.float32
NT = (((1,), (1,)), ((), ()))
NN = (((1,), (0,)), ((), ()))
TN = (((0,), (0,)), ((), ()))


def dot(a, b, dims):
    return lax.dot_general(a, b, dims, preferred_element_type=F32)


def kernel(
    rows_total, q_ref, k_ref, v_ref, g_ref, lse_ref, delta_ref, fin_dq, fin_dkv,
    sent, got, stats, halo, halo_grad, halo_in, acc,
    dq_buf, dkv_buf, xq, xl, xacc, xdq, xd_in, chain, local, local_stats, ready, s_in, s_own,
    s_split, r_split, s_st, r_st, s_hf, r_hf, s_hb, r_hb,
    s_dq, r_dq, s_dkv, r_dkv, s_xq, r_xq, s_xl, r_xl, s_xd, r_xd,
):
    rows, heads, dim = q_ref.shape
    hpg = heads // GROUP
    half = 2 * rows
    last = rows_total - 1
    scale = dim ** -0.5
    log2e = math.log2(math.e)

    s, h = lax.axis_index("seq"), lax.axis_index("head")
    lo, m = s % 2, s // 2
    hi, core = h // 2, h % 2
    place = lo * 4 + hi * 2 + core
    mine = hi * 4 + core * 2 + lo

    def peer(o):
        lo2, hi2, core2 = (lo + o % 2) % 2, (hi + o // 2 % 2) % 2, (core + o // 4) % 2
        return (2 * m + lo2, hi2 * 2 + core2), lo2 * 4 + hi2 * 2 + core2, hi2 * 4 + core2 * 2 + lo2

    peers = [(o, *peer(o)) for o in (2, 3, 1, 6, 7, 5, 4)]

    def row(step):
        return (2 * ((m + step + rows_total) % rows_total) + lo, h)

    def copy(src, dst, send, recv, to):
        return pltpu.make_async_remote_copy(
            src_ref=src, dst_ref=dst, send_sem=send, recv_sem=recv, device_id=to, device_id_type=MESH
        )

    kv_buf, qg_buf = got.at[0], got.at[1]

    def split_copy(kind, i, o, to, place2, mine2):
        return copy(
            sent.at[kind, mine2, i], got.at[kind, i, place], s_split.at[kind, i, o - 1], r_split.at[kind, i, o - 1], to
        )

    def split_arrived(kind, i, part):
        @pl.when(hi == part)
        def _():
            for p in peers:
                if p[0] in (1, 4, 5):
                    split_copy(kind, i, *p).wait_recv()

        @pl.when(hi != part)
        def _():
            for p in peers:
                if p[0] not in (1, 4, 5):
                    split_copy(kind, i, *p).wait_recv()

    def dq_copy(i, o, to, place2, mine2):
        return copy(dq_buf.at[i, place2], fin_dq.at[mine, i], s_dq.at[i, o - 1], r_dq.at[i, o - 1], to)

    def dkv_copy(i, o, to, place2, mine2):
        return copy(dkv_buf.at[i, place2], fin_dkv.at[mine, i], s_dkv.at[i, o - 1], r_dkv.at[i, o - 1], to)

    def keep(i):
        return (
            pltpu.make_async_copy(dq_buf.at[i, place], fin_dq.at[mine, i], s_own.at[i, 0]),
            pltpu.make_async_copy(dkv_buf.at[i, place], fin_dkv.at[mine, i], s_own.at[i, 1]),
        )

    def stat_copy():
        return copy(stats.at[lo], stats.at[lo], s_st.at[0], r_st.at[0], peer(1)[0])

    def halo_copy(i, n):
        src = halo.at[i, 2] if n == 0 else kv_buf.at[i, pl.ds((0, 4)[n - 1], 2)]
        return copy(src, halo.at[i, n], s_hf.at[i, n], r_hf.at[i, n], row(1))

    def back_copy(i, n):
        return copy(halo_grad.at[i, n], halo_in.at[i, n], s_hb.at[i, n], r_hb.at[i, n], row(-1))

    def xq_copy(i, n):
        second_half = qg_buf.at[i, pl.ds((2, 6, 2)[n], 2)]
        slot = (0, 1, 2 * (m % 2))[n]
        return copy(second_half, xq.at[i, slot], s_xq.at[i, n], r_xq.at[i, slot], row((-1, -1, -2)[n]))

    def xq_arrived(i, slot):
        to = xq.at[i, slot]
        return copy(to, to, s_xq.at[i, 0], r_xq.at[i, slot], row(1))

    def xl_copy(n):
        slot = (m % 2, 0)[n]
        return copy(stats, xl.at[slot], s_xl.at[n], r_xl.at[slot], row((-2, -1)[n]))

    def xl_arrived(slot):
        return copy(xl.at[slot], xl.at[slot], s_xl.at[0], r_xl.at[slot], row(1))

    def xd_copy(i, n):
        slot = (0, 1, 2 * ((m - (rows_total - 2)) % 2))[n]
        return copy(xdq.at[i, slot], xd_in.at[i, n], s_xd.at[i, n], r_xd.at[i, n], row((1, 1, 2)[n]))

    def load_of(n, src=k_ref):
        return pltpu.make_async_copy(src, local.at[n], s_in.at[n])

    stat_loads = [
        pltpu.make_async_copy(src, local_stats.at[n], s_in.at[4 + n]) for n, src in enumerate((lse_ref, delta_ref))
    ]
    for n, src in enumerate((k_ref, v_ref, q_ref, g_ref)):
        load_of(n, src).start()
    for load in stat_loads:
        load.start()

    barrier = pltpu.get_barrier_semaphore()
    for _, to, _, _ in peers:
        pl.semaphore_signal(barrier, inc=1, device_id=to, device_id_type=MESH)

    def tell(sem, step):
        pl.semaphore_signal(sem, inc=1, device_id=row(step), device_id_type=MESH)

    @pl.when(m <= last - 1)
    def _():
        tell(barrier, 1)

    @pl.when(m >= 1)
    def _():
        tell(barrier, -1)

    @pl.when(m <= 1)
    def _():
        tell(barrier, -2)

    @pl.when(m == 0)
    def _():
        tell(barrier, -1)

    def split_heads(kind):
        for which in range(2):
            load_of(2 * kind + which).wait()
            by_head = jnp.swapaxes(local[2 * kind + which], 0, 1)
            sent[kind, :, :, which] = by_head.reshape(GROUP, hpg, rows, dim)
        got[kind, :, pl.ds(place, 1)] = sent[kind, mine][:, None]

    first, second = hi, 1 - hi
    split_heads(first)
    for load in stat_loads:
        load.wait()
    stats[lo, 0] = local_stats[0] * log2e
    stats[lo, 1] = local_stats[1]

    one, none = jnp.int32(1), jnp.int32(0)
    along = jnp.where(m >= 1, one, none) + jnp.where(m <= last - 1, one, none)
    ends = jnp.where(m >= last - 1, one, none) + jnp.where(m == last, one, none)
    pl.semaphore_wait(barrier, GROUP - 1 + along + ends)

    @pl.when(m >= last - 1)
    def _():
        tell(ready, 2)

    @pl.when(m == last)
    def _():
        tell(ready, 1)

    stat_copy().start()

    def send(kind, i):
        for p in peers:
            split_copy(kind, i, *p).start()

    @pl.loop(0, 2)
    def _(i):
        send(first, i)

    split_heads(second)

    @pl.loop(0, hpg - 2)
    def _(i):
        send(second, i)
        send(first, i + 2)

    @pl.loop(hpg - 2, hpg)
    def _(i):
        send(second, i)

    acc[...] = jnp.zeros_like(acc)

    @pl.when(m <= 1)
    def _():
        halo[:, 0] = jnp.zeros_like(halo[:, 0])

    @pl.when(m == 0)
    def _():
        halo[:, 1:3] = jnp.zeros_like(halo[:, 1:3])

    @pl.when(m == last)
    def _():
        halo_in[...] = jnp.zeros_like(halo_in)

    def hand_on(i):
        @pl.when(m >= 1)
        def _():
            halo_copy(i, 2).wait_recv()

            @pl.when(m <= last - 1)
            def _():
                halo_copy(i, 0).start()

    def share_keys(i):
        split_arrived(0, i, 0)

        @pl.when(m <= last - 1)
        def _():
            halo_copy(i, 2).start()
            halo_copy(i, 1).start()

    def share_queries(i):
        split_arrived(1, i, 1)

        @pl.when(m == 0)
        def _():
            xq_copy(i, 0).start()
            xq_copy(i, 1).start()

        @pl.when(m == 1)
        def _():
            xq_copy(i, 2).start()

        @pl.when((m == 0) & (i >= 1))
        def _():
            xq_copy(i - 1, 2).start()

        @pl.when((m == 0) & (i == hpg - 1))
        def _():
            xq_copy(i, 2).start()

    @pl.loop(0, 2)
    def _(i):
        share_keys(i)

    stat_copy().wait_recv()

    @pl.when(m <= 1)
    def _():
        pl.semaphore_wait(ready, 2 - m)
        xl_copy(0).start()

    @pl.when(m == 0)
    def _():
        xl_copy(1).start()

    @pl.loop(0, 2)
    def _(i):
        share_queries(i)

    @pl.loop(0, 2)
    def _(i):
        hand_on(i)

    key_at = lax.broadcasted_iota(jnp.int32, (half, half), 0)
    query_at = lax.broadcasted_iota(jnp.int32, (half, half), 1)
    causal = key_at <= query_at

    def flat(x):
        return x.reshape(-1, dim)

    def tile(kk, vv, qq, gg, lse, delta):
        scores = dot(kk, qq, NT) * (scale * log2e) - lse
        return jnp.exp2(scores), dot(vv, gg, NT) - delta

    def compute(i):
        keys = [halo[i, :, :, 0], kv_buf[i, 0:2, 0], kv_buf[i, 4:6, 0]]
        vals = [halo[i, :, :, 1], kv_buf[i, 0:2, 1], kv_buf[i, 4:6, 1]]
        keys = jnp.concatenate([flat(x) for x in keys], axis=0)
        vals = jnp.concatenate([flat(x) for x in vals], axis=0)
        at = pl.ds(4 * lo + i, 1)
        parts = []
        for b in range(2):
            kk, vv = keys[b * half : (b + 4) * half], vals[b * half : (b + 4) * half]
            k2, v2 = flat(kv_buf[i, 4 * b + 2 : 4 * b + 4, 0]), flat(kv_buf[i, 4 * b + 2 : 4 * b + 4, 1])
            qq, gg = flat(qg_buf[i, 4 * b : 4 * b + 4, 0]), flat(qg_buf[i, 4 * b : 4 * b + 4, 1])
            lse, delta = stats[b, 0, at, :], stats[b, 1, at, :]
            probs, pgrad = tile(kk, vv, qq, gg, lse, delta)
            own = probs[3 * half :]
            own = jnp.concatenate([jnp.where(causal, own[:, :half], 0.0), own[:, half:]], axis=1)
            probs = jnp.concatenate([probs[: 3 * half], own], axis=0)
            sgrad = (probs * pgrad).astype(BF16)
            dv = dot(probs.astype(BF16), gg, NN)
            dk = dot(sgrad, qq, NN) * scale
            q2, g2 = qq[half:], gg[half:]
            probs, pgrad = tile(k2, v2, q2, g2, lse[:, half:], delta[:, half:])
            probs = jnp.where(causal, probs, 0.0)
            sgrad2 = (probs * pgrad).astype(BF16)
            acc[i, b, 1, 1] += dot(probs.astype(BF16), g2, NN)
            acc[i, b, 1, 0] += dot(sgrad2, q2, NN) * scale
            dq = dot(sgrad, kk, TN)
            dq = jnp.concatenate([dq[:half], dq[half:] + dot(sgrad2, k2, TN)], axis=0) * scale
            dq_buf[i, 4 * b : 4 * b + 4] = dq.astype(BF16).reshape(4, rows, dim)
            parts.append((dk, dv))
        for which in range(2):
            e, o = parts[0][which], parts[1][which]
            halo_grad[i, 0, which] = e[:half].astype(BF16)
            halo_grad[i, 1, which] = (e[half : 2 * half] + o[:half]).astype(BF16)
            chain[i, which] = e[2 * half : 3 * half] + o[half : 2 * half]
            acc[i, 0, 0, which] += e[3 * half :] + o[2 * half : 3 * half]
            acc[i, 1, 0, which] += o[3 * half :]

    def wrapped(i, slot, b, first):
        kk, vv = flat(kv_buf[i, 4 * b : 4 * b + 4, 0]), flat(kv_buf[i, 4 * b : 4 * b + 4, 1])
        qq, gg = flat(xq[i, slot, :, 0]), flat(xq[i, slot, :, 1])
        at = pl.ds(4 * lo + i, 1)
        lse = xl[slot // 2, slot % 2, 0, at, :][:, half:]
        delta = xl[slot // 2, slot % 2, 1, at, :][:, half:]
        probs, pgrad = tile(kk, vv, qq, gg, lse, delta)
        sgrad = (probs * pgrad).astype(BF16)
        dv = dot(probs.astype(BF16), gg, NN)
        dk = dot(sgrad, qq, NN) * scale
        for part in range(2):
            cut = slice(part * half, (part + 1) * half)
            acc[i, b, part, 0] += dk[cut]
            acc[i, b, part, 1] += dv[cut]
        dq = dot(sgrad, kk, TN) * scale
        if first:
            xacc[slot] = dq
        else:
            xacc[slot] += dq

    def send_dq(i):
        for p in peers:
            dq_copy(i, *p).start()

    def send_dq_part(i, part):
        for p in peers:

            @pl.when(p[2] // 2 % 2 == part)
            def _(p=p):
                dq_copy(i, *p).start()

    def pass_back(i):
        @pl.when(m >= 1)
        def _():
            @pl.when(m <= last - 1)
            def _():
                back_copy(i, 0).wait_recv()

            halo_grad[i, 2] = (chain[i] + halo_in[i, 0].astype(F32)).astype(BF16)
            back_copy(i, 2).start()

    def wrapped_last(i):
        @pl.when(m == last)
        def _():
            for slot in range(3):
                xq_arrived(i, slot).wait_recv()
            for slot in range(2):
                wrapped(i, slot, 0, True)
            wrapped(i, 2, 1, True)
            for slot in range(2):
                wrapped(i, slot, 1, False)
            xdq[i] = xacc[...].astype(BF16)
            for n in range(3):
                xd_copy(i, n).start()

    def wrapped_one(i):
        @pl.when(m == last - 1)
        def _():
            xq_arrived(i, 0).wait_recv()
            wrapped(i, 0, 1, True)
            xdq[i, 0] = xacc[0].astype(BF16)
            xd_copy(i, 2).start()

    def finish(i):
        @pl.when(m <= last - 1)
        def _():
            back_copy(i, 1).wait_recv()
            back_copy(i, 2).wait_recv()

        for which in range(2):
            for b in range(2):
                first = acc[i, b, 0, which] + halo_in[i, 1 + b, which].astype(F32)
                dkv_buf[i, 4 * b : 4 * b + 2, which] = first.astype(BF16).reshape(2, rows, dim)
                second = acc[i, b, 1, which]
                dkv_buf[i, 4 * b + 2 : 4 * b + 4, which] = second.astype(BF16).reshape(2, rows, dim)
        for p in peers:
            dkv_copy(i, *p).start()

    def finish_first(i):
        xd_copy(i, 2).wait_recv()
        more = xd_in[i, 2].astype(F32).reshape(2, rows, dim)
        dq_buf[i, 2:4] = (dq_buf[i, 2:4].astype(F32) + more).astype(BF16)

        @pl.when(m == 0)
        def _():
            for slot in range(2):
                xd_copy(i, slot).wait_recv()
                at = slice(4 * slot + 2, 4 * slot + 4)
                more = xd_in[i, slot].astype(F32).reshape(2, rows, dim)
                dq_buf[i, at] = (dq_buf[i, at].astype(F32) + more).astype(BF16)

        send_dq_part(i, 1)

    @pl.when(m == last)
    def _():
        xl_arrived(0).wait_recv()
        xl_arrived(1).wait_recv()

    @pl.when(m == last - 1)
    def _():
        xl_arrived(0).wait_recv()

    def grads(i):
        split_arrived(1, i, 0)
        @pl.when(m >= 2)
        def _():
            halo_copy(i, 0).wait_recv()

        @pl.when(m >= 1)
        def _():
            halo_copy(i, 1).wait_recv()

        compute(i)

        @pl.when(m >= 2)
        def _():
            back_copy(i, 0).start()

        @pl.when(m >= 1)
        def _():
            back_copy(i, 1).start()

        @pl.when(m >= 2)
        def _():
            send_dq(i)

        @pl.when(m <= 1)
        def _():
            send_dq_part(i, 0)

    @pl.loop(0, hpg)
    def _(i):
        split_arrived(0, i, 1)
        wrapped_last(i)
        grads(i)

        @pl.when((i >= 1) & (i + 1 < hpg))
        def _():
            hand_on(i + 1)

        @pl.when(i >= 1)
        def _():
            pass_back(i - 1)

        @pl.when(i + 2 < hpg)
        def _():
            share_keys(i + 2)
            share_queries(i + 2)

        @pl.when(i >= 1)
        def _():
            wrapped_one(i - 1)

    wrapped_one(hpg - 1)

    @pl.loop(0, hpg)
    def _(i):
        finish(i)

        @pl.when(i == 0)
        def _():
            pass_back(hpg - 1)

        @pl.when((m <= 1) & (i >= 2))
        def _():
            finish_first(i - 2)

    @pl.when(m <= 1)
    def _():
        @pl.loop(hpg - 2, hpg)
        def _(i):
            finish_first(i)

    @pl.loop(0, hpg)
    def _(i):
        own_dq, own_dkv = keep(i)
        own_dq.start()
        own_dkv.start()

    @pl.loop(0, hpg)
    def _(i):
        for p in peers:
            dq_copy(i, *p).wait_recv()
            dkv_copy(i, *p).wait_recv()
        own_dq, own_dkv = keep(i)
        own_dq.wait()
        own_dkv.wait()

    stat_copy().wait_send()

    @pl.loop(0, hpg)
    def _(i):
        for p in peers:
            for kind in range(2):
                split_copy(kind, i, *p).wait_send()
            dq_copy(i, *p).wait_send()
            dkv_copy(i, *p).wait_send()

        @pl.when(m <= last - 1)
        def _():
            halo_copy(i, 1).wait_send()
            halo_copy(i, 2).wait_send()

            @pl.when(m >= 1)
            def _():
                halo_copy(i, 0).wait_send()

        @pl.when(m >= 2)
        def _():
            back_copy(i, 0).wait_send()

        @pl.when(m >= 1)
        def _():
            back_copy(i, 1).wait_send()
            back_copy(i, 2).wait_send()

        @pl.when(m == 0)
        def _():
            xq_copy(i, 0).wait_send()
            xq_copy(i, 1).wait_send()

        @pl.when(m <= 1)
        def _():
            xq_copy(i, 2).wait_send()

        @pl.when(m >= last - 1)
        def _():
            xd_copy(i, 2).wait_send()

        @pl.when(m == last)
        def _():
            xd_copy(i, 0).wait_send()
            xd_copy(i, 1).wait_send()

    @pl.when(m <= 1)
    def _():
        xl_copy(0).wait_send()

    @pl.when(m == 0)
    def _():
        xl_copy(1).wait_send()


PARTS = 2


def join_heads(dq_ref, dkv_ref, dq_out, dk_out, dv_out, by_head, by_row, s_load, s_store):
    groups, hpg, rows, dim = dq_ref.shape
    size = rows // PARTS
    loads, stores = [], []
    for n, src in enumerate((dq_ref, dkv_ref.at[:, :, 0], dkv_ref.at[:, :, 1])):
        for part in range(PARTS):
            cut = pl.ds(part * size, size)
            loads.append(pltpu.make_async_copy(src.at[:, :, cut], by_head.at[n, :, :, cut], s_load.at[n, part]))
            loads[-1].start()
    for n, dst in enumerate((dq_out, dk_out, dv_out)):
        for part in range(PARTS):
            cut = pl.ds(part * size, size)
            loads[n * PARTS + part].wait()
            block = by_head[n, :, :, part * size : (part + 1) * size].reshape(groups * hpg, size, dim)
            by_row[n, part * size : (part + 1) * size] = jnp.swapaxes(block, 0, 1)
            stores.append(pltpu.make_async_copy(by_row.at[n, cut], dst.at[cut], s_store.at[n, part]))
            stores[-1].start()
    for store in stores:
        store.wait()


def on_device(queries, key_vectors, value_vectors, grad_output, logsumexp, row_delta):
    rows, heads, dim = queries.shape
    hpg = heads // GROUP
    half = 2 * rows
    rows_total = lax.axis_size("seq") // 2
    hbm = pl.BlockSpec(memory_space=pl.ANY)
    dma = pltpu.SemaphoreType.DMA
    dq_shape = jax.ShapeDtypeStruct((GROUP, hpg, rows, dim), BF16)
    dkv_shape = jax.ShapeDtypeStruct((GROUP, hpg, 2, rows, dim), BF16)

    def body(*refs):
        kernel(rows_total, *refs)

    dq, dkv = pl.pallas_call(
        body,
        out_shape=(dq_shape, dkv_shape),
        in_specs=[hbm] * 6,
        out_specs=(hbm, hbm),
        scratch_shapes=[
            pltpu.VMEM((2, GROUP, hpg, 2, rows, dim), BF16),
            pltpu.VMEM((2, hpg, GROUP, 2, rows, dim), BF16),
            pltpu.VMEM((2, 2, *logsumexp.shape), F32),
            pltpu.VMEM((hpg, 3, 2, 2, rows, dim), BF16),
            pltpu.VMEM((hpg, 3, 2, half, dim), BF16),
            pltpu.VMEM((hpg, 3, 2, half, dim), BF16),
            pltpu.VMEM((hpg, 2, 2, 2, half, dim), F32),
            pltpu.VMEM((hpg, GROUP, rows, dim), BF16),
            pltpu.VMEM((hpg, GROUP, 2, rows, dim), BF16),
            pltpu.VMEM((hpg, 3, 2, 2, rows, dim), BF16),
            pltpu.VMEM((2, 2, 2, *logsumexp.shape), F32),
            pltpu.VMEM((3, half, dim), F32),
            pltpu.VMEM((hpg, 3, half, dim), BF16),
            pltpu.VMEM((hpg, 3, half, dim), BF16),
            pltpu.VMEM((hpg, 2, half, dim), F32),
            pltpu.VMEM((4, rows, heads, dim), BF16),
            pltpu.VMEM((2, *logsumexp.shape), F32),
            pltpu.SemaphoreType.REGULAR,
            dma((6,)),
            dma((hpg, 2)),
            *[dma((2, hpg, GROUP - 1))] * 2,
            *[dma((1,))] * 2,
            *[dma((hpg, 3))] * 4,
            *[dma((hpg, GROUP - 1))] * 4,
            *[dma((hpg, 3))] * 2,
            *[dma((2,))] * 2,
            *[dma((hpg, 3))] * 2,
        ],
        compiler_params=pltpu.CompilerParams(
            collective_id=0, has_side_effects=True, vmem_limit_bytes=60 << 20
        ),
        name="window_grads",
    )(queries, key_vectors, value_vectors, grad_output, logsumexp, row_delta)

    out = jax.ShapeDtypeStruct((rows, heads, dim), BF16)
    return pl.pallas_call(
        join_heads,
        out_shape=(out, out, out),
        in_specs=[hbm] * 2,
        out_specs=(hbm, hbm, hbm),
        scratch_shapes=[
            pltpu.VMEM((3, GROUP, hpg, rows, dim), BF16),
            pltpu.VMEM((3, rows, heads, dim), BF16),
            dma((3, PARTS)),
            dma((3, PARTS)),
        ],
        compiler_params=pltpu.CompilerParams(vmem_limit_bytes=60 << 20),
        name="join_heads",
    )(dq, dkv)


def solution(mesh):
    rows = P(("seq", "head"), None, None)
    stats = P("head", "seq")
    return jax.shard_map(
        on_device,
        mesh=mesh,
        in_specs=(rows, rows, rows, rows, stats, stats),
        out_specs=(rows, rows, rows),
        check_vma=False,
    )
```
